1024 devices in a mesh: outer: 32 (over x, y_hi, core), inner: 32 (over y_lo, z).
Axes of the slice: x: 4, y: 8 (y_hi: 4, y_lo: 2; y = y_hi * 2 + y_lo), z: 16, core: 2. Of those that a mesh axis runs over, the one named last changes fastest.
Arguments:
- image_embed: bfloat16 [16384, 1152], P(('outer', 'inner')), may hold values from -1 to 1, as said below
- text_embed: bfloat16 [16384, 1152], P(('outer', 'inner')), may hold values from -1 to 1, as said below
- labels: int32 [16384], P(('outer', 'inner')), may hold values from 0 to 8191
- log_temp: float32 [1], replicated, may hold values from 0.5 to 1.5
- bias: float32 [1], replicated, may hold values from -2 to 0
Outputs:
- grad_image: float32 [16384, 1152], P(('outer', 'inner'))
- grad_text: float32 [16384, 1152], P(('outer', 'inner'))
- row_loss: float32 [16384], P(('outer', 'inner'))
The draws below stay inside these ranges and needn't reach their ends.
Inputs may be any that keep to these rules, and one draw needn't show every extreme that they name: `image_embed`: embedding rows of varied length. `text_embed`: embedding rows of varied length.
All inputs are finite; a program needn't handle non-finite values.
Results may differ from the reference program's by a relative error of at most 0.0036.
Values may be sent and summed in bfloat16 or wider, within the bound.
No kernel may reach another device: no remote copies, remote signals or barrier semaphores. Data moves between devices by JAX's collectives and lax.ppermute only.
A program may use at most 32 MiB of HBM per device.

```python
import math
import jax
import jax.numpy as jnp
from jax import lax

D = 1152
TOKENS = 16384
N_OUTER = 32


def shape_rows(base, row_key, col_key):
    rows = jnp.exp(jax.random.uniform(row_key, (TOKENS, 1), minval=math.log(0.3), maxval=math.log(3.0)))
    cols = jnp.exp(jax.random.uniform(col_key, (1, D), minval=-0.6, maxval=0.6))
    values = jnp.clip(base * rows * cols / math.sqrt(D), -1.0, 1.0)
    return values.astype(jnp.bfloat16)


def draw_image_embed(key, part):
    key = jax.random.fold_in(key, 11)
    base_key, row_key, col_key = jax.random.split(key, 3)
    base = jnp.clip(jax.random.normal(base_key, (TOKENS, D)), -6.0, 6.0)
    return shape_rows(base, row_key, col_key)


def draw_text_embed(key, part):
    key = jax.random.fold_in(key, 23)
    base_key, row_key, col_key = jax.random.split(key, 3)
    base = jnp.clip(jax.random.normal(base_key, (TOKENS, D)), -6.0, 6.0)
    return shape_rows(base, row_key, col_key)


def with_ends(array, key, low, top_value):
    shape = array.shape
    spot = [jax.random.randint(jax.random.fold_in(key, axis), (), 0, shape[axis]) for axis in range(len(shape))]
    array = array.at[tuple(spot)].set(low)
    longest = shape.index(max(shape))
    spot[longest] = (spot[longest] + 1) % shape[longest]
    return array.at[tuple(spot)].set(top_value)


def setup_inputs(seed: int = 0) -> dict:
    splits = jax.random.split(jax.random.key(seed), 6)
    return {
        "image_embed": draw_image_embed(jax.random.fold_in(splits[5], 71), 0),
        "text_embed": draw_text_embed(jax.random.fold_in(splits[5], 71), 0),
        "labels": with_ends(jax.random.randint(splits[2], (TOKENS,), 0, TOKENS // 2), jax.random.fold_in(splits[2], 1), 0, (TOKENS // 2) - 1).astype(jnp.int32),
        "log_temp": jnp.clip(jax.random.uniform(splits[3], (1,), jnp.float32, 0.5, 1.5), 0.5, 1.5),
        "bias": jnp.clip(jax.random.uniform(splits[4], (1,), jnp.float32, -2.0, 0.0), -2.0, 0.0),
    }


def normalize(embed):
    values = embed.astype(jnp.float32)
    radius = jnp.sqrt(lax.optimization_barrier(jnp.sum(values * values, axis=1, keepdims=True)) + 1e-06)
    return (values / radius, radius)

def unproject(unit, radius, grad):
    return (grad - unit * lax.optimization_barrier(jnp.sum(unit * grad, axis=1, keepdims=True))) / radius

def contract(left, right, left_dim, right_dim):
    return lax.dot_general(left, right, (((left_dim,), (right_dim,)), ((), ())), preferred_element_type=jnp.float32)

def reference(image_embed, text_embed, labels, log_temp, bias):
    image_unit, image_radius = normalize(image_embed)
    text_unit, text_radius = normalize(text_embed)
    image_low = image_unit.astype(jnp.bfloat16)
    text_low = text_unit.astype(jnp.bfloat16)
    scale_now = jnp.exp(log_temp[0])
    offset = bias[0]
    image_blocks = image_low.reshape(N_OUTER, -1, D)
    label_blocks = labels.reshape(N_OUTER, -1)

    def visit(text_total, block):
        image_part, label_part = block
        scores = scale_now * contract(image_part, text_low, 1, 1) + offset
        positive = label_part[:, None] == labels[None, :]
        losses = lax.optimization_barrier(jnp.sum(jax.nn.softplus(jnp.where(positive, -scores, scores)), axis=1)) / TOKENS
        coeffs = (jax.nn.sigmoid(scores) - positive.astype(jnp.float32)).astype(jnp.bfloat16)
        image_part_grad = scale_now * contract(coeffs, text_low, 1, 0)
        text_total = text_total + scale_now * contract(coeffs, image_part, 0, 0)
        return (text_total, (image_part_grad, losses))
    start = jnp.zeros((TOKENS, D), jnp.float32)
    text_unit_grad, outputs = lax.scan(visit, start, (image_blocks, label_blocks))
    image_unit_grad = outputs[0].reshape(TOKENS, D)
    row_loss = outputs[1].reshape(TOKENS)
    grad_image = unproject(image_unit, image_radius, image_unit_grad)
    grad_text = unproject(text_unit, text_radius, text_unit_grad)
    return (grad_image, grad_text, row_loss)
```

```python
import jax
import jax.numpy as jnp
from jax import lax
from jax.sharding import Mesh, PartitionSpec as P

AXES = ("x", "y_hi", "core", "y_lo", "z")
PLANE = ("x", "y_hi", "y_lo")
WIDTH = 1152


def normalize(embed):
    values = embed.astype(jnp.float32)
    radius = jnp.sqrt(jnp.sum(values * values, axis=1, keepdims=True) + 1e-06)
    return (values / radius, radius)


def unproject(unit, radius, grad):
    return (grad - unit * jnp.sum(unit * grad, axis=1, keepdims=True)) / radius


def contract(left, right, left_dim, right_dim):
    return lax.dot_general(
        left, right, (((left_dim,), (right_dim,)), ((), ())), preferred_element_type=jnp.float32
    )


def label_columns(labels):
    high, low = labels // 128, labels % 128
    columns = jnp.stack([high, low], axis=1).astype(jnp.bfloat16)
    return jnp.pad(columns, ((0, 0), (0, 126)))


def label_of(columns):
    part = columns[:, WIDTH : WIDTH + 2].astype(jnp.int32)
    return part[:, 0] * 128 + part[:, 1]


def spread(block, axes):
    copies = lax.axis_size(axes)
    out = jnp.broadcast_to(block[None], (copies,) + block.shape)
    return lax.all_to_all(out, axes, 0, 0, tiled=True).reshape(-1, block.shape[1])


def swap_cores(part):
    return lax.ppermute(part, "core", [(0, 1), (1, 0)])


def on_device(image_embed, text_embed, labels, log_temp, bias):
    image_unit, image_radius = normalize(image_embed)
    text_unit, text_radius = normalize(text_embed)
    marks = label_columns(labels)
    image_low = jnp.concatenate([image_unit.astype(jnp.bfloat16), marks], axis=1)
    text_low = jnp.concatenate([text_unit.astype(jnp.bfloat16), marks], axis=1)
    scale_now = jnp.exp(log_temp[0])
    offset = bias[0]
    rows_here = image_embed.shape[0]
    total = rows_here * lax.axis_size(AXES)

    mine = spread(image_low, "z")
    group_text = spread(text_low, PLANE)
    group_image = jnp.concatenate([mine, swap_cores(mine)], axis=0)

    scores = scale_now * contract(group_image[:, :WIDTH], group_text[:, :WIDTH], 1, 1) + offset
    positive = label_of(group_image)[:, None] == label_of(group_text)[None, :]
    loss_part = jnp.sum(jax.nn.softplus(jnp.where(positive, -scores, scores)), axis=1)
    coeffs = (jax.nn.sigmoid(scores) - positive.astype(jnp.float32)).astype(jnp.bfloat16)

    image_part = contract(coeffs, group_text[:, :WIDTH], 1, 0)
    text_part = contract(coeffs, group_image[:, :WIDTH], 0, 0).astype(jnp.bfloat16)
    loss_high = loss_part.astype(jnp.bfloat16)
    loss_low = (loss_part - loss_high.astype(jnp.float32)).astype(jnp.bfloat16)
    loss_cols = jnp.pad(jnp.stack([loss_high, loss_low], axis=1), ((0, 0), (0, 126))).astype(jnp.float32)
    image_part = jnp.concatenate([image_part, loss_cols], axis=1)

    half = image_part.shape[0] // 2
    other = swap_cores(image_part[half:].astype(jnp.bfloat16))
    other = other.astype(jnp.float32)
    got_loss = jnp.sum(other[:, WIDTH : WIDTH + 2], axis=1) + loss_part[:half]
    both = (image_part[:half, :WIDTH] + other[:, :WIDTH]).astype(jnp.bfloat16)
    loss_high = got_loss.astype(jnp.bfloat16)
    loss_low = (got_loss - loss_high.astype(jnp.float32)).astype(jnp.bfloat16)
    loss_cols = jnp.pad(jnp.stack([loss_high, loss_low], axis=1), ((0, 0), (0, 126)))
    both = jnp.concatenate([both, loss_cols], axis=1)
    text_terms = lax.all_to_all(text_part.reshape(-1, rows_here, WIDTH), PLANE, 0, 0, tiled=True)
    image_terms = lax.all_to_all(both.reshape(-1, rows_here, WIDTH + 128), "z", 0, 0, tiled=True)

    text_sum = scale_now * jnp.sum(text_terms.astype(jnp.float32), axis=0)
    image_sum = jnp.sum(image_terms.astype(jnp.float32), axis=0)
    row_loss = jnp.sum(image_sum[:, WIDTH : WIDTH + 2], axis=1) / total
    grad_image = unproject(image_unit, image_radius, scale_now * image_sum[:, :WIDTH])
    grad_text = unproject(text_unit, text_radius, text_sum)
    return (grad_image, grad_text, row_loss)


def solution(mesh):
    parts = Mesh(mesh.devices.reshape(4, 4, 2, 2, 16), AXES)
    placed = (P(AXES, None), P(AXES, None), P(AXES), P(), P())
    return jax.shard_map(
        on_device,
        mesh=parts,
        in_specs=placed,
        out_specs=(P(AXES, None), P(AXES, None), P(AXES)),
        check_vma=False,
    )
```

```python
import functools

import jax
import jax.numpy as jnp
from jax import lax
from jax.experimental import pallas as pl
from jax.experimental.pallas import tpu as pltpu
from jax.sharding import Mesh, PartitionSpec as P

AXES = ("x", "y_hi", "core", "y_lo", "z_hi", "z_lo")
PLANE = ("x", "y_hi", "y_lo")
COLUMN = ("z_hi", "z_lo")
WIDTH = 1152
WIDE = WIDTH + 128
ROWS = 16
LABEL_BASE = 128
F32, BF16 = jnp.float32, jnp.bfloat16

VMEM = pl.BlockSpec(memory_space=pltpu.VMEM)
SMEM = pl.BlockSpec(memory_space=pltpu.SMEM)


def call(kernel, out_shape, in_specs, flops=0, bytes_accessed=0):
    many = isinstance(out_shape, (list, tuple))
    return pl.pallas_call(
        kernel,
        out_shape=out_shape,
        in_specs=in_specs,
        out_specs=[VMEM] * len(out_shape) if many else VMEM,
        compiler_params=pltpu.CompilerParams(vmem_limit_bytes=20 * 1024 * 1024),
        cost_estimate=pl.CostEstimate(
            flops=flops, bytes_accessed=bytes_accessed, transcendentals=0
        ),
    )


def unit_of(embed):
    values = embed.astype(F32)
    radius = jnp.sqrt(jnp.sum(values * values, axis=1, keepdims=True) + 1e-06)
    return values / radius, radius


def prepare(labels_ref, image_ref, text_ref, image_out, text_out):
    shape = (ROWS, 128)
    row = lax.broadcasted_iota(jnp.int32, shape, 0)
    lane = lax.broadcasted_iota(jnp.int32, shape, 1)
    label = jnp.zeros(shape, jnp.int32)
    for r in range(ROWS):
        label = jnp.where(row == r, labels_ref[r], label)
    high, low = label >> 7, label & (LABEL_BASE - 1)
    norm = high * high + low * low
    norm_high, norm_low = norm >> 7, norm & (LABEL_BASE - 1)

    def features(values):
        out = jnp.zeros(shape, jnp.int32)
        for k, value in enumerate(values):
            out = jnp.where(lane == k, value, out)
        return out.astype(F32).astype(BF16)

    image_out[:, :WIDTH] = unit_of(image_ref[...])[0].astype(BF16)
    image_out[:, WIDTH:] = features((-2 * high, -2 * low, norm_high, norm_low, LABEL_BASE, 1))
    text_low = unit_of(text_ref[...])[0].astype(BF16)
    marks = features((high, low, LABEL_BASE, 1, norm_high, norm_low))
    for k in range(text_out.shape[0]):
        text_out[k, :, :WIDTH] = text_low
        text_out[k, :, WIDTH:] = marks


def dot(left, right, left_dim, right_dim):
    return lax.dot_general(
        left, right, (((left_dim,), (right_dim,)), ((), ())), preferred_element_type=F32
    )


def loss_pair(loss):
    lane = lax.broadcasted_iota(jnp.int32, (loss.shape[0], 128), 1)
    high = loss.astype(BF16).astype(F32)
    return jnp.where(lane == 0, high, jnp.where(lane == 1, loss - high, 0.0)).astype(BF16)


def tile(log_temp_ref, bias_ref, mine_ref, other_ref, text_ref, keep_out, give_out, text_out):
    scale = jnp.exp(jnp.full((1, 1), log_temp_ref[0], F32))
    bias = bias_ref[0]
    text = text_ref[:, :WIDTH]
    marks = text_ref[:, WIDTH:]
    total = None
    for half, image_ref in enumerate((mine_ref, other_ref)):
        image = image_ref[:, :WIDTH]
        scores = scale * dot(image, text, 1, 1) + bias
        positive = dot(image_ref[:, WIDTH:], marks, 1, 1) == 0.0
        small = jnp.exp(-jnp.abs(scores))
        losses = jnp.maximum(jnp.where(positive, -scores, scores), 0.0) + jnp.log1p(small)
        loss = jnp.sum(losses, axis=1, keepdims=True)
        sigmoid = jnp.where(scores >= 0.0, 1.0, small) / (1.0 + small)
        coeffs = (sigmoid - jnp.where(positive, 1.0, 0.0)).astype(BF16)
        part = dot(coeffs, text, 1, 0)
        if half == 0:
            lane = lax.broadcasted_iota(jnp.int32, (loss.shape[0], 128), 1)
            keep_out[:, :WIDTH] = part
            keep_out[:, WIDTH:] = jnp.where(lane == 0, loss, 0.0)
        else:
            give_out[:, :WIDTH] = part.astype(BF16)
            give_out[:, WIDTH:] = loss_pair(loss)
        back = dot(coeffs, image, 0, 0)
        total = back if total is None else total + back
    text_out[...] = total.astype(BF16)


def merged(keep_ref, got_ref, rows):
    body = keep_ref[rows, :WIDTH] + got_ref[rows, :WIDTH].astype(F32)
    loss = jnp.sum(
        keep_ref[rows, WIDTH:] + got_ref[rows, WIDTH:].astype(F32), axis=1, keepdims=True
    )
    return body, loss


def fold(side_ref, keep_ref, got_ref, keep_out, *give_outs):
    side = side_ref[0]
    size = len(give_outs) + 1
    lane = lax.broadcasted_iota(jnp.int32, (ROWS, 128), 1)
    for group in range(keep_out.shape[0] // ROWS):
        out = pl.ds(group * ROWS, ROWS)
        for shift in range(size):
            place = lax.rem(side + shift, size)
            body, loss = merged(keep_ref, got_ref, pl.ds((size * group + place) * ROWS, ROWS))
            if shift == 0:
                keep_out[out, :WIDTH] = body
                keep_out[out, WIDTH:] = jnp.where(lane == 0, loss, 0.0)
            else:
                give_outs[shift - 1][out, :WIDTH] = body.astype(BF16)
                give_outs[shift - 1][out, WIDTH:] = loss_pair(loss)


def last_fold(keep_ref, *refs):
    got_refs, out_ref = refs[:-2], refs[-1]
    for block in range(out_ref.shape[0]):
        rows = pl.ds(block * ROWS, ROWS)
        terms = keep_ref[rows, :]
        for got_ref in got_refs:
            terms += got_ref[rows, :].astype(F32)
        out_ref[block, :, :WIDTH] = terms[:, :WIDTH].astype(BF16)
        out_ref[block, :, WIDTH:] = loss_pair(jnp.sum(terms[:, WIDTH:], axis=1, keepdims=True))


def unproject(log_temp_ref, embed_ref, terms):
    scale = jnp.exp(jnp.full((1, 1), log_temp_ref[0], F32))
    unit, radius = unit_of(embed_ref[...])
    grad = scale * terms
    return (grad - unit * jnp.sum(unit * grad, axis=1, keepdims=True)) / radius


def finish_text(log_temp_ref, embed_ref, terms_ref, grad_out):
    terms = terms_ref[0].astype(F32)
    for k in range(1, terms_ref.shape[0]):
        terms += terms_ref[k].astype(F32)
    grad_out[...] = unproject(log_temp_ref, embed_ref, terms)


def finish_image(total, log_temp_ref, embed_ref, terms_ref, grad_out, loss_out):
    terms = terms_ref[0].astype(F32)
    for k in range(1, terms_ref.shape[0]):
        terms += terms_ref[k].astype(F32)
    grad_out[...] = unproject(log_temp_ref, embed_ref, terms[:, :WIDTH])
    loss = jnp.sum(terms[:, WIDTH:], axis=1, keepdims=True) / total
    row = lax.broadcasted_iota(jnp.int32, (ROWS, 128), 0)
    lane = lax.broadcasted_iota(jnp.int32, (ROWS, 128), 1)
    loss_out[...] = jnp.sum(jnp.where(row == lane, loss, 0.0), axis=0, keepdims=True)[:, :ROWS]


def swap_cores(part):
    return lax.ppermute(part, "core", [(0, 1), (1, 0)])


def on_device(image_embed, text_embed, labels, log_temp, bias):
    total = ROWS * lax.axis_size(AXES)
    plane, column = lax.axis_size(PLANE), lax.axis_size(COLUMN)
    shape = jax.ShapeDtypeStruct

    image_wide, text_wide = call(
        prepare,
        [shape((ROWS, WIDE), BF16), shape((plane, ROWS, WIDE), BF16)],
        [SMEM, VMEM, VMEM],
        bytes_accessed=plane * ROWS * WIDE * 2,
    )(labels, image_embed, text_embed)

    group_text = lax.all_to_all(text_wide, PLANE, 0, 0, tiled=True).reshape(-1, WIDE)
    mine = lax.all_gather(image_wide, COLUMN, axis=0, tiled=True)
    other = swap_cores(mine)

    half, texts = column * ROWS, plane * ROWS
    keep, give, text_part = call(
        tile,
        [shape((half, WIDE), F32), shape((half, WIDE), BF16), shape((texts, WIDTH), BF16)],
        [SMEM, SMEM, VMEM, VMEM, VMEM],
        flops=12 * half * texts * WIDTH,
        bytes_accessed=8 * texts * WIDE,
    )(log_temp, bias, mine, other, group_text)

    text_terms = lax.all_to_all(text_part.reshape(plane, ROWS, WIDTH), PLANE, 0, 0, tiled=True)

    got = swap_cores(give)
    side = lax.axis_index("z_lo").astype(jnp.int32).reshape(1)
    size, blocks = lax.axis_size("z_lo"), lax.axis_size("z_hi")
    rows = blocks * ROWS
    keep, *gives = call(
        fold,
        [shape((rows, WIDE), F32)] + [shape((rows, WIDE), BF16)] * (size - 1),
        [SMEM, VMEM, VMEM],
        bytes_accessed=32 * rows * WIDE,
    )(side, keep, got)
    gots = [
        lax.ppermute(give, "z_lo", [(i, (i + shift) % size) for i in range(size)])
        for shift, give in enumerate(gives, 1)
    ]
    image_terms = call(
        last_fold,
        shape((blocks, ROWS, WIDE), BF16),
        [VMEM] * size + [pl.BlockSpec(memory_space=pl.ANY)],
        bytes_accessed=12 * rows * WIDE,
    )(keep, *gots, text_terms)
    image_terms = lax.all_to_all(image_terms, "z_hi", 0, 0, tiled=True)

    grad_text = call(
        finish_text, shape((ROWS, WIDTH), F32), [SMEM, VMEM, VMEM], bytes_accessed=2 * texts * WIDTH
    )(log_temp, text_embed, text_terms)
    grad_image, loss = call(
        functools.partial(finish_image, total),
        [shape((ROWS, WIDTH), F32), shape((1, ROWS), F32)],
        [SMEM, VMEM, VMEM],
        bytes_accessed=2 * blocks * ROWS * WIDE,
    )(log_temp, image_embed, image_terms)
    return (grad_image, grad_text, loss.reshape(ROWS))


def solution(mesh):
    parts = Mesh(mesh.devices.reshape(4, 4, 2, 2, 4, 4), AXES)
    placed = (P(AXES, None), P(AXES, None), P(AXES), P(), P())
    return jax.shard_map(
        on_device,
        mesh=parts,
        in_specs=placed,
        out_specs=(P(AXES, None), P(AXES, None), P(AXES)),
        check_vma=False,
    )
```

```python
import functools

import jax
import jax.numpy as jnp
from jax import lax
from jax.experimental import pallas as pl
from jax.experimental.pallas import tpu as pltpu
from jax.sharding import Mesh, PartitionSpec as P

AXES = ("x", "y_hi", "core", "y_lo", "z_hi", "z_lo")
PLANE = ("x", "y_hi", "y_lo")
COLUMN = ("z_hi", "z_lo")
WIDTH = 1152
WIDE = WIDTH + 128
ROWS = 16
LABEL_BASE = 128
F32, BF16 = jnp.float32, jnp.bfloat16

VMEM = pl.BlockSpec(memory_space=pltpu.VMEM)
SMEM = pl.BlockSpec(memory_space=pltpu.SMEM)
HBM = pl.BlockSpec(memory_space=pltpu.HBM)


def call(kernel, outs, in_specs, scratch=(), flops=0, bytes_accessed=0, vmem=16):
    return pl.pallas_call(
        kernel,
        out_shape=[
            pltpu.HBM(shape.shape, shape.dtype) if spec is HBM else shape for spec, shape in outs
        ],
        in_specs=in_specs,
        out_specs=[spec for spec, _ in outs],
        scratch_shapes=list(scratch),
        compiler_params=pltpu.CompilerParams(vmem_limit_bytes=vmem * 1024 * 1024),
        cost_estimate=pl.CostEstimate(
            flops=flops, bytes_accessed=bytes_accessed, transcendentals=0
        ),
    )


def start(*copies):
    for copy in copies:
        copy.start()
    return copies


def wait(*copies):
    for copy in copies:
        copy.wait()


def unit_of(embed):
    values = embed.astype(F32)
    radius = jnp.sqrt(jnp.sum(values * values, axis=1, keepdims=True) + 1e-06)
    return values / radius, radius


def prepare(
    labels_ref, image_ref, text_ref, image_out, text_out, labels_now, image_now, text_now, text_wide, in_sem, out_sem
):
    labels_copy, image_copy, text_copy = start(
        pltpu.make_async_copy(labels_ref, labels_now, in_sem.at[0]),
        pltpu.make_async_copy(image_ref, image_now, in_sem.at[1]),
        pltpu.make_async_copy(text_ref, text_now, in_sem.at[2]),
    )
    wait(labels_copy)
    shape = (ROWS, 128)
    row = lax.broadcasted_iota(jnp.int32, shape, 0)
    lane = lax.broadcasted_iota(jnp.int32, shape, 1)
    label = jnp.zeros(shape, jnp.int32)
    for r in range(ROWS):
        label = jnp.where(row == r, labels_now[r], label)
    high, low = label >> 7, label & (LABEL_BASE - 1)
    norm = high * high + low * low
    norm_high, norm_low = norm >> 7, norm & (LABEL_BASE - 1)

    def features(values):
        out = jnp.zeros(shape, jnp.int32)
        for k, value in enumerate(values):
            out = jnp.where(lane == k, value, out)
        return out.astype(F32).astype(BF16)

    wait(text_copy)
    text_wide[:, :WIDTH] = unit_of(text_now[...])[0].astype(BF16)
    text_wide[:, WIDTH:] = features((high, low, LABEL_BASE, 1, norm_high, norm_low))
    copies = start(
        *[
            pltpu.make_async_copy(text_wide, text_out.at[k], out_sem.at[k])
            for k in range(text_out.shape[0])
        ]
    )
    wait(image_copy)
    image_out[:, :WIDTH] = unit_of(image_now[...])[0].astype(BF16)
    image_out[:, WIDTH:] = features((-2 * high, -2 * low, norm_high, norm_low, LABEL_BASE, 1))
    wait(*copies)


def dot(left, right, left_dim, right_dim):
    return lax.dot_general(
        left, right, (((left_dim,), (right_dim,)), ((), ())), preferred_element_type=F32
    )


def loss_pair(loss):
    lane = lax.broadcasted_iota(jnp.int32, (loss.shape[0], 128), 1)
    high = loss.astype(BF16).astype(F32)
    return jnp.where(lane == 0, high, jnp.where(lane == 1, loss - high, 0.0)).astype(BF16)


def half_tile(log_temp_ref, bias_ref, wide, text_wide):
    scale = jnp.exp(jnp.full((1, 1), log_temp_ref[0], F32))
    scores = scale * dot(wide[:, :WIDTH], text_wide[:, :WIDTH], 1, 1) + bias_ref[0]
    positive = dot(wide[:, WIDTH:], text_wide[:, WIDTH:], 1, 1) == 0.0
    small = jnp.exp(-jnp.abs(scores))
    losses = jnp.maximum(jnp.where(positive, -scores, scores), 0.0) + jnp.log1p(small)
    sigmoid = jnp.where(scores >= 0.0, 1.0, small) / (1.0 + small)
    coeffs = (sigmoid - jnp.where(positive, 1.0, 0.0)).astype(BF16)
    return jnp.sum(losses, axis=1, keepdims=True), coeffs


def first_tile(
    log_temp_ref, bias_ref, mine_ref, text_ref, coeffs_out, keep_out, mine, text, coeffs_now, keep_now, in_sem, out_sem
):
    wait(
        *start(
            pltpu.make_async_copy(mine_ref, mine, in_sem.at[0]),
            pltpu.make_async_copy(text_ref, text, in_sem.at[1]),
        )
    )
    loss, coeffs = half_tile(log_temp_ref, bias_ref, mine, text)
    coeffs_now[...] = coeffs
    (coeffs_copy,) = start(pltpu.make_async_copy(coeffs_now, coeffs_out, out_sem.at[0]))
    lane = lax.broadcasted_iota(jnp.int32, (loss.shape[0], 128), 1)
    keep_now[:, :WIDTH] = dot(coeffs, text[:, :WIDTH], 1, 0)
    keep_now[:, WIDTH:] = jnp.where(lane == 0, loss, 0.0)
    (keep_copy,) = start(pltpu.make_async_copy(keep_now, keep_out, out_sem.at[1]))
    wait(coeffs_copy, keep_copy)


def second_tile(
    order, log_temp_ref, bias_ref, other_ref, text_ref, mine_ref, coeffs_ref, give_out, text_out,
    other, text, mine, mine_coeffs, coeffs_now, give_now, text_now, in_sem, out_sem
):
    other_copy, text_copy, mine_copy, coeffs_copy = start(
        pltpu.make_async_copy(other_ref, other, in_sem.at[0]),
        pltpu.make_async_copy(text_ref, text, in_sem.at[1]),
        pltpu.make_async_copy(mine_ref, mine, in_sem.at[2]),
        pltpu.make_async_copy(coeffs_ref, mine_coeffs, in_sem.at[3]),
    )
    wait(other_copy, text_copy)
    loss, coeffs = half_tile(log_temp_ref, bias_ref, other, text)
    coeffs_now[...] = coeffs
    give_now[:, :WIDTH] = dot(coeffs, text[:, :WIDTH], 1, 0).astype(BF16)
    give_now[:, WIDTH:] = loss_pair(loss)
    copies = list(start(pltpu.make_async_copy(give_now, give_out, out_sem.at[0])))
    wait(mine_copy, coeffs_copy)
    chunk = 8
    for first in range(0, len(order), chunk):
        columns = pl.ds(first * ROWS, chunk * ROWS)
        total = dot(mine_coeffs[:, columns], mine[:, :WIDTH], 0, 0)
        total += dot(coeffs_now[:, columns], other[:, :WIDTH], 0, 0)
        for k in range(chunk):
            place = order[first + k]
            text_now[place] = total[k * ROWS : (k + 1) * ROWS].astype(BF16)
            copies += start(
                pltpu.make_async_copy(text_now.at[place], text_out.at[place], out_sem.at[1 + place])
            )
    wait(*copies)


def merged(keep_ref, got_ref, rows):
    body = keep_ref[rows, :WIDTH] + got_ref[rows, :WIDTH].astype(F32)
    loss = jnp.sum(
        keep_ref[rows, WIDTH:] + got_ref[rows, WIDTH:].astype(F32), axis=1, keepdims=True
    )
    return body, loss


def fold(side_ref, keep_ref, got_ref, keep_out, *give_outs):
    side = side_ref[0]
    size = len(give_outs) + 1
    lane = lax.broadcasted_iota(jnp.int32, (ROWS, 128), 1)
    for group in range(keep_out.shape[0] // ROWS):
        out = pl.ds(group * ROWS, ROWS)
        for shift in range(size):
            place = lax.rem(side + shift, size)
            body, loss = merged(keep_ref, got_ref, pl.ds((size * group + place) * ROWS, ROWS))
            if shift == 0:
                keep_out[out, :WIDTH] = body
                keep_out[out, WIDTH:] = jnp.where(lane == 0, loss, 0.0)
            else:
                give_outs[shift - 1][out, :WIDTH] = body.astype(BF16)
                give_outs[shift - 1][out, WIDTH:] = loss_pair(loss)


def last_fold(keep_ref, *refs):
    got_refs, out_ref = refs[:-2], refs[-1]
    for block in range(out_ref.shape[0]):
        rows = pl.ds(block * ROWS, ROWS)
        terms = keep_ref[rows, :]
        for got_ref in got_refs:
            terms += got_ref[rows, :].astype(F32)
        out_ref[block, :, :WIDTH] = terms[:, :WIDTH].astype(BF16)
        out_ref[block, :, WIDTH:] = loss_pair(jnp.sum(terms[:, WIDTH:], axis=1, keepdims=True))


def unproject(log_temp_ref, embed_ref, terms):
    scale = jnp.exp(jnp.full((1, 1), log_temp_ref[0], F32))
    unit, radius = unit_of(embed_ref[...])
    grad = scale * terms
    return (grad - unit * jnp.sum(unit * grad, axis=1, keepdims=True)) / radius


def fold_text(bit_ref, terms_ref, keep_out, give_out):
    bit = bit_ref[0]
    for pair in range(keep_out.shape[0]):
        for out_ref, place in ((keep_out, bit), (give_out, 1 - bit)):
            terms = terms_ref[0, 2 * pair + place].astype(F32)
            for k in range(1, terms_ref.shape[0]):
                terms += terms_ref[k, 2 * pair + place].astype(F32)
            out_ref[pair] = terms.astype(out_ref.dtype)


def fold_text_again(bit_ref, keep_ref, got_ref, keep_out, give_out):
    bit = bit_ref[0]
    keep_out[...] = keep_ref[bit] + got_ref[bit].astype(F32)
    give_out[...] = (keep_ref[1 - bit] + got_ref[1 - bit].astype(F32)).astype(BF16)


def finish_text(log_temp_ref, embed_ref, keep_ref, got_ref, grad_out):
    terms = keep_ref[...] + got_ref[...].astype(F32)
    grad_out[...] = unproject(log_temp_ref, embed_ref, terms)


def finish_image(total, log_temp_ref, embed_ref, terms_ref, grad_out, loss_out):
    terms = terms_ref[0].astype(F32)
    for k in range(1, terms_ref.shape[0]):
        terms += terms_ref[k].astype(F32)
    grad_out[...] = unproject(log_temp_ref, embed_ref, terms[:, :WIDTH])
    loss = jnp.sum(terms[:, WIDTH:], axis=1, keepdims=True) / total
    row = lax.broadcasted_iota(jnp.int32, (ROWS, 128), 0)
    lane = lax.broadcasted_iota(jnp.int32, (ROWS, 128), 1)
    loss_out[...] = jnp.sum(jnp.where(row == lane, loss, 0.0), axis=0, keepdims=True)[:, :ROWS]


def in_hbm(array):
    return pltpu.with_memory_space_constraint(array, pltpu.HBM)


def place_of(axis):
    return lax.axis_index(axis).astype(jnp.int32).reshape(1)


def swap_cores(part):
    return lax.ppermute(part, "core", [(0, 1), (1, 0)])


def on_device(image_embed, text_embed, labels, log_temp, bias):
    total = ROWS * lax.axis_size(AXES)
    plane, column = lax.axis_size(PLANE), lax.axis_size(COLUMN)
    shape = jax.ShapeDtypeStruct

    image_wide, text_wide = call(
        prepare,
        [(VMEM, shape((ROWS, WIDE), BF16)), (HBM, shape((plane, ROWS, WIDE), BF16))],
        [HBM, HBM, HBM],
        [
            pltpu.SMEM((ROWS,), jnp.int32),
            pltpu.VMEM((ROWS, WIDTH), BF16),
            pltpu.VMEM((ROWS, WIDTH), BF16),
            pltpu.VMEM((ROWS, WIDE), BF16),
            pltpu.SemaphoreType.DMA((3,)),
            pltpu.SemaphoreType.DMA((plane,)),
        ],
        bytes_accessed=plane * ROWS * WIDE * 2,
    )(in_hbm(labels), in_hbm(image_embed), in_hbm(text_embed))

    group_text = lax.all_to_all(text_wide, PLANE, 0, 0, tiled=True).reshape(-1, WIDE)
    mine = lax.all_gather(image_wide, COLUMN, axis=0, tiled=True)
    other = swap_cores(mine)

    half, texts = column * ROWS, plane * ROWS

    coeffs, keep = call(
        first_tile,
        [(HBM, shape((half, texts), BF16)), (HBM, shape((half, WIDE), F32))],
        [SMEM, SMEM, HBM, HBM],
        [
            pltpu.VMEM((half, WIDE), BF16),
            pltpu.VMEM((texts, WIDE), BF16),
            pltpu.VMEM((half, texts), BF16),
            pltpu.VMEM((half, WIDE), F32),
            pltpu.SemaphoreType.DMA((2,)),
            pltpu.SemaphoreType.DMA((2,)),
        ],
        flops=4 * half * texts * WIDTH,
        bytes_accessed=4 * texts * WIDE,
    )(log_temp, bias, mine, group_text)

    far, low = lax.axis_size("y_hi"), lax.axis_size("y_lo")
    near = plane // far
    order = [((b // low // far) * low + b % low) * far + (b // low) % far for b in range(plane)]
    give, text_part = call(
        functools.partial(second_tile, order),
        [(HBM, shape((half, WIDE), BF16)), (HBM, shape((plane, ROWS, WIDTH), BF16))],
        [SMEM, SMEM, HBM, HBM, HBM, HBM],
        [
            pltpu.VMEM((half, WIDE), BF16),
            pltpu.VMEM((texts, WIDE), BF16),
            pltpu.VMEM((half, WIDE), BF16),
            pltpu.VMEM((half, texts), BF16),
            pltpu.VMEM((half, texts), BF16),
            pltpu.VMEM((half, WIDE), BF16),
            pltpu.VMEM((plane, ROWS, WIDTH), BF16),
            pltpu.SemaphoreType.DMA((4,)),
            pltpu.SemaphoreType.DMA((plane + 1,)),
        ],
        flops=8 * half * texts * WIDTH,
        bytes_accessed=6 * texts * WIDE,
    )(log_temp, bias, other, group_text, mine, coeffs)

    text_terms = lax.all_to_all(text_part, ("x", "y_lo"), 0, 0, tiled=True)
    text_terms = text_terms.reshape(near, far, ROWS, WIDTH)
    place = lax.axis_index("y_hi").astype(jnp.int32)
    text_keep, text_give = call(
        fold_text,
        [(VMEM, shape((far // 2, ROWS, WIDTH), F32)), (VMEM, shape((far // 2, ROWS, WIDTH), BF16))],
        [SMEM, VMEM],
        bytes_accessed=3 * texts * WIDTH,
    )((place % 2).reshape(1), text_terms)
    text_got = lax.ppermute(text_give, "y_hi", [(i, i ^ 1) for i in range(far)])
    first_got = text_got
    text_keep, text_give = call(
        fold_text_again,
        [(VMEM, shape((ROWS, WIDTH), F32)), (VMEM, shape((ROWS, WIDTH), BF16))],
        [SMEM, VMEM, VMEM],
        bytes_accessed=10 * ROWS * WIDTH,
    )((place // 2).reshape(1), text_keep, text_got)
    text_got = lax.ppermute(text_give, "y_hi", [(i, i ^ 2) for i in range(far)])

    got = swap_cores(give)
    side = lax.axis_index("z_lo").astype(jnp.int32).reshape(1)
    size, blocks = lax.axis_size("z_lo"), lax.axis_size("z_hi")
    rows = blocks * ROWS
    keep, *gives = call(
        fold,
        [(VMEM, shape((rows, WIDE), F32))] + [(VMEM, shape((rows, WIDE), BF16))] * (size - 1),
        [SMEM, VMEM, VMEM],
        bytes_accessed=32 * rows * WIDE,
    )(side, keep, got)
    gots = [
        lax.ppermute(give, "z_lo", [(i, (i + shift) % size) for i in range(size)])
        for shift, give in enumerate(gives, 1)
    ]
    (image_terms,) = call(
        last_fold,
        [(VMEM, shape((blocks, ROWS, WIDE), BF16))],
        [VMEM] * size + [HBM],
        bytes_accessed=12 * rows * WIDE,
    )(keep, *gots, first_got)
    image_terms = lax.all_to_all(image_terms, "z_hi", 0, 0, tiled=True)

    (grad_text,) = call(
        finish_text,
        [(VMEM, shape((ROWS, WIDTH), F32))],
        [SMEM, VMEM, VMEM, VMEM],
        bytes_accessed=12 * ROWS * WIDTH,
    )(log_temp, text_embed, text_keep, text_got)
    grad_image, loss = call(
        functools.partial(finish_image, total),
        [(VMEM, shape((ROWS, WIDTH), F32)), (VMEM, shape((1, ROWS), F32))],
        [SMEM, VMEM, VMEM],
        bytes_accessed=2 * blocks * ROWS * WIDE,
    )(log_temp, image_embed, image_terms)
    return (grad_image, grad_text, loss.reshape(ROWS))


def solution(mesh):
    parts = Mesh(mesh.devices.reshape(4, 4, 2, 2, 4, 4), AXES)
    placed = (P(AXES, None), P(AXES, None), P(AXES), P(), P())
    return jax.shard_map(
        on_device,
        mesh=parts,
        in_specs=placed,
        out_specs=(P(AXES, None), P(AXES, None), P(AXES)),
        check_vma=False,
    )
```

```python
import functools

import jax
import jax.numpy as jnp
from jax import lax
from jax.experimental import pallas as pl
from jax.experimental.pallas import tpu as pltpu
from jax.sharding import Mesh, PartitionSpec as P

AXES = ("x", "y_hi", "core", "y_lo", "z_hi", "z_lo")
PLANE = ("x", "y_hi", "y_lo")
COLUMN = ("z_hi", "z_lo")
WIDTH = 1152
WIDE = WIDTH + 128
ROWS = 16
LABEL_BASE = 128
F32, BF16 = jnp.float32, jnp.bfloat16

VMEM = pl.BlockSpec(memory_space=pltpu.VMEM)
SMEM = pl.BlockSpec(memory_space=pltpu.SMEM)
HBM = pl.BlockSpec(memory_space=pltpu.HBM)


def call(kernel, outs, in_specs, scratch=(), flops=0, bytes_accessed=0, vmem=16):
    return pl.pallas_call(
        kernel,
        out_shape=[
            pltpu.HBM(shape.shape, shape.dtype) if spec is HBM else shape for spec, shape in outs
        ],
        in_specs=in_specs,
        out_specs=[spec for spec, _ in outs],
        scratch_shapes=list(scratch),
        compiler_params=pltpu.CompilerParams(vmem_limit_bytes=vmem * 1024 * 1024),
        cost_estimate=pl.CostEstimate(
            flops=flops, bytes_accessed=bytes_accessed, transcendentals=0
        ),
    )


def start(*copies):
    for copy in copies:
        copy.start()
    return copies


def wait(*copies):
    for copy in copies:
        copy.wait()


def unit_of(embed):
    values = embed.astype(F32)
    radius = jnp.sqrt(jnp.sum(values * values, axis=1, keepdims=True) + 1e-06)
    return values / radius, radius


def prepare(
    labels_ref, image_ref, text_ref, image_out, text_out, labels_now, image_now, text_now, text_wide, in_sem, out_sem
):
    labels_copy, image_copy, text_copy = start(
        pltpu.make_async_copy(labels_ref, labels_now, in_sem.at[0]),
        pltpu.make_async_copy(image_ref, image_now, in_sem.at[1]),
        pltpu.make_async_copy(text_ref, text_now, in_sem.at[2]),
    )
    wait(labels_copy)
    shape = (ROWS, 128)
    row = lax.broadcasted_iota(jnp.int32, shape, 0)
    lane = lax.broadcasted_iota(jnp.int32, shape, 1)
    label = jnp.zeros(shape, jnp.int32)
    for r in range(ROWS):
        label = jnp.where(row == r, labels_now[r], label)
    high, low = label >> 7, label & (LABEL_BASE - 1)
    norm = high * high + low * low
    norm_high, norm_low = norm >> 7, norm & (LABEL_BASE - 1)

    def features(values):
        out = jnp.zeros(shape, jnp.int32)
        for k, value in enumerate(values):
            out = jnp.where(lane == k, value, out)
        return out.astype(F32).astype(BF16)

    wait(text_copy)
    text_wide[:, :WIDTH] = unit_of(text_now[...])[0].astype(BF16)
    text_wide[:, WIDTH:] = features((high, low, LABEL_BASE, 1, norm_high, norm_low))
    copies = start(
        *[
            pltpu.make_async_copy(text_wide, text_out.at[k], out_sem.at[k])
            for k in range(text_out.shape[0])
        ]
    )
    wait(image_copy)
    image_out[:, :WIDTH] = unit_of(image_now[...])[0].astype(BF16)
    image_out[:, WIDTH:] = features((-2 * high, -2 * low, norm_high, norm_low, LABEL_BASE, 1))
    wait(*copies)


def dot(left, right, left_dim, right_dim):
    return lax.dot_general(
        left, right, (((left_dim,), (right_dim,)), ((), ())), preferred_element_type=F32
    )


def loss_pair(loss):
    lane = lax.broadcasted_iota(jnp.int32, (loss.shape[0], 128), 1)
    high = loss.astype(BF16).astype(F32)
    return jnp.where(lane == 0, high, jnp.where(lane == 1, loss - high, 0.0)).astype(BF16)


def half_tile(log_temp_ref, bias_ref, wide, text_wide):
    scale = jnp.exp(jnp.full((1, 1), log_temp_ref[0], F32))
    scores = scale * dot(wide[:, :WIDTH], text_wide[:, :WIDTH], 1, 1) + bias_ref[0]
    positive = dot(wide[:, WIDTH:], text_wide[:, WIDTH:], 1, 1) == 0.0
    small = jnp.exp(-jnp.abs(scores))
    losses = jnp.maximum(jnp.where(positive, -scores, scores), 0.0) + jnp.log1p(small)
    sigmoid = jnp.where(scores >= 0.0, 1.0, small) / (1.0 + small)
    coeffs = (sigmoid - jnp.where(positive, 1.0, 0.0)).astype(BF16)
    return jnp.sum(losses, axis=1, keepdims=True), coeffs


def first_tile(
    log_temp_ref, bias_ref, mine_ref, text_ref, coeffs_out, keep_out, mine, text, coeffs_now, keep_now, in_sem, out_sem
):
    wait(
        *start(
            pltpu.make_async_copy(mine_ref, mine, in_sem.at[0]),
            pltpu.make_async_copy(text_ref, text, in_sem.at[1]),
        )
    )
    loss, coeffs = half_tile(log_temp_ref, bias_ref, mine, text)
    coeffs_now[...] = coeffs
    (coeffs_copy,) = start(pltpu.make_async_copy(coeffs_now, coeffs_out, out_sem.at[0]))
    keep_now[:, :WIDTH] = dot(coeffs, text[:, :WIDTH], 1, 0)
    keep_now[:, WIDTH:] = loss_lane(loss)
    (keep_copy,) = start(pltpu.make_async_copy(keep_now, keep_out, out_sem.at[1]))
    wait(coeffs_copy, keep_copy)


def second_tile(
    order, log_temp_ref, bias_ref, other_ref, text_ref, mine_ref, coeffs_ref, give_out, text_out,
    other, text, mine, mine_coeffs, coeffs_now, give_now, text_now, in_sem, out_sem
):
    other_copy, text_copy, mine_copy, coeffs_copy = start(
        pltpu.make_async_copy(other_ref, other, in_sem.at[0]),
        pltpu.make_async_copy(text_ref, text, in_sem.at[1]),
        pltpu.make_async_copy(mine_ref, mine, in_sem.at[2]),
        pltpu.make_async_copy(coeffs_ref, mine_coeffs, in_sem.at[3]),
    )
    wait(other_copy, text_copy)
    loss, coeffs = half_tile(log_temp_ref, bias_ref, other, text)
    coeffs_now[...] = coeffs
    give_now[:, :WIDTH] = dot(coeffs, text[:, :WIDTH], 1, 0).astype(BF16)
    give_now[:, WIDTH:] = loss_pair(loss)
    copies = list(start(pltpu.make_async_copy(give_now, give_out, out_sem.at[0])))
    wait(mine_copy, coeffs_copy)
    chunk = 8
    for first in range(0, len(order), chunk):
        columns = pl.ds(first * ROWS, chunk * ROWS)
        total = dot(mine_coeffs[:, columns], mine[:, :WIDTH], 0, 0)
        total += dot(coeffs_now[:, columns], other[:, :WIDTH], 0, 0)
        for k in range(chunk):
            place = order[first + k]
            text_now[place] = total[k * ROWS : (k + 1) * ROWS].astype(BF16)
            copies += start(
                pltpu.make_async_copy(text_now.at[place], text_out.at[place], out_sem.at[1 + place])
            )
    wait(*copies)


def loss_lane(loss):
    lane = lax.broadcasted_iota(jnp.int32, (loss.shape[0], 128), 1)
    return jnp.where(lane == 0, loss, 0.0)


def fold(bit_ref, keep_ref, got_ref, keep_out, left_out, right_out):
    bit = bit_ref[0]
    split = left_out.shape[1]
    for pair in range(keep_out.shape[0] // ROWS):
        out = pl.ds(pair * ROWS, ROWS)
        for place in (bit, 1 - bit):
            rows = pl.ds((2 * pair + place) * ROWS, ROWS)
            terms = keep_ref[rows, :] + got_ref[rows, :].astype(F32)
            loss = jnp.sum(terms[:, WIDTH:], axis=1, keepdims=True)
            if place is bit:
                keep_out[out, :WIDTH] = terms[:, :WIDTH]
                keep_out[out, WIDTH:] = loss_lane(loss)
            else:
                left_out[out, :] = terms[:, :split].astype(BF16)
                right_out[out, : WIDTH - split] = terms[:, split:WIDTH].astype(BF16)
                right_out[out, WIDTH - split :] = loss_pair(loss)


def last_fold(keep_ref, left_ref, right_ref, part_out, out_ref, out_sem):
    copies = []
    split = left_ref.shape[1]
    for block in range(out_ref.shape[0]):
        rows = pl.ds(block * ROWS, ROWS)
        out_ref[block, :, :split] = (keep_ref[rows, :split] + left_ref[rows, :].astype(F32)).astype(BF16)
        terms = keep_ref[rows, split:] + right_ref[rows, :].astype(F32)
        out_ref[block, :, split:WIDTH] = terms[:, : WIDTH - split].astype(BF16)
        loss = jnp.sum(terms[:, WIDTH - split :], axis=1, keepdims=True)
        out_ref[block, :, WIDTH:] = loss_pair(loss)
        copies += start(
            pltpu.make_async_copy(out_ref.at[block], part_out.at[block], out_sem.at[block])
        )
    wait(*copies)


def unproject(log_temp_ref, embed_ref, terms):
    scale = jnp.exp(jnp.full((1, 1), log_temp_ref[0], F32))
    unit, radius = unit_of(embed_ref[...])
    grad = scale * terms
    return (grad - unit * jnp.sum(unit * grad, axis=1, keepdims=True)) / radius


def fold_text(bit_ref, terms_ref, keep_out, give_out):
    bit = bit_ref[0]
    for pair in range(keep_out.shape[0]):
        for out_ref, place in ((keep_out, bit), (give_out, 1 - bit)):
            terms = terms_ref[0, 2 * pair + place].astype(F32)
            for k in range(1, terms_ref.shape[0]):
                terms += terms_ref[k, 2 * pair + place].astype(F32)
            out_ref[pair] = terms.astype(out_ref.dtype)


def fold_text_again(bit_ref, keep_ref, got_ref, keep_out, give_out):
    bit = bit_ref[0]
    keep_out[...] = keep_ref[bit] + got_ref[bit].astype(F32)
    give_out[...] = (keep_ref[1 - bit] + got_ref[1 - bit].astype(F32)).astype(BF16)


def finish_text(log_temp_ref, embed_ref, keep_ref, got_ref, grad_out):
    terms = keep_ref[...] + got_ref[...].astype(F32)
    grad_out[...] = unproject(log_temp_ref, embed_ref, terms)


def finish_image(total, log_temp_ref, embed_ref, terms_ref, grad_out, loss_out):
    terms = terms_ref[0].astype(F32)
    for k in range(1, terms_ref.shape[0]):
        terms += terms_ref[k].astype(F32)
    grad_out[...] = unproject(log_temp_ref, embed_ref, terms[:, :WIDTH])
    loss = jnp.sum(terms[:, WIDTH:], axis=1, keepdims=True) / total
    row = lax.broadcasted_iota(jnp.int32, (ROWS, 128), 0)
    lane = lax.broadcasted_iota(jnp.int32, (ROWS, 128), 1)
    loss_out[...] = jnp.sum(jnp.where(row == lane, loss, 0.0), axis=0, keepdims=True)[:, :ROWS]


def in_hbm(array):
    return pltpu.with_memory_space_constraint(array, pltpu.HBM)


def place_of(axis):
    return lax.axis_index(axis).astype(jnp.int32).reshape(1)


def swap_cores(part):
    return lax.ppermute(part, "core", [(0, 1), (1, 0)])


def on_device(image_embed, text_embed, labels, log_temp, bias):
    total = ROWS * lax.axis_size(AXES)
    plane, column = lax.axis_size(PLANE), lax.axis_size(COLUMN)
    shape = jax.ShapeDtypeStruct

    image_wide, text_wide = call(
        prepare,
        [(VMEM, shape((ROWS, WIDE), BF16)), (HBM, shape((plane, ROWS, WIDE), BF16))],
        [HBM, HBM, HBM],
        [
            pltpu.SMEM((ROWS,), jnp.int32),
            pltpu.VMEM((ROWS, WIDTH), BF16),
            pltpu.VMEM((ROWS, WIDTH), BF16),
            pltpu.VMEM((ROWS, WIDE), BF16),
            pltpu.SemaphoreType.DMA((3,)),
            pltpu.SemaphoreType.DMA((plane,)),
        ],
        bytes_accessed=plane * ROWS * WIDE * 2,
    )(in_hbm(labels), in_hbm(image_embed), in_hbm(text_embed))

    group_text = lax.all_to_all(text_wide, PLANE, 0, 0, tiled=True).reshape(-1, WIDE)
    mine = lax.all_gather(image_wide, COLUMN, axis=0, tiled=True)
    other = swap_cores(mine)

    half, texts = column * ROWS, plane * ROWS

    coeffs, keep = call(
        first_tile,
        [(HBM, shape((half, texts), BF16)), (HBM, shape((half, WIDE), F32))],
        [SMEM, SMEM, HBM, HBM],
        [
            pltpu.VMEM((half, WIDE), BF16),
            pltpu.VMEM((texts, WIDE), BF16),
            pltpu.VMEM((half, texts), BF16),
            pltpu.VMEM((half, WIDE), F32),
            pltpu.SemaphoreType.DMA((2,)),
            pltpu.SemaphoreType.DMA((2,)),
        ],
        flops=4 * half * texts * WIDTH,
        bytes_accessed=4 * texts * WIDE,
    )(log_temp, bias, mine, group_text)

    far, low = lax.axis_size("y_hi"), lax.axis_size("y_lo")
    near = plane // far
    order = [((b // low // far) * low + b % low) * far + (b // low) % far for b in range(plane)]
    give, text_part = call(
        functools.partial(second_tile, order),
        [(HBM, shape((half, WIDE), BF16)), (HBM, shape((plane, ROWS, WIDTH), BF16))],
        [SMEM, SMEM, HBM, HBM, HBM, HBM],
        [
            pltpu.VMEM((half, WIDE), BF16),
            pltpu.VMEM((texts, WIDE), BF16),
            pltpu.VMEM((half, WIDE), BF16),
            pltpu.VMEM((half, texts), BF16),
            pltpu.VMEM((half, texts), BF16),
            pltpu.VMEM((half, WIDE), BF16),
            pltpu.VMEM((plane, ROWS, WIDTH), BF16),
            pltpu.SemaphoreType.DMA((4,)),
            pltpu.SemaphoreType.DMA((plane + 1,)),
        ],
        flops=8 * half * texts * WIDTH,
        bytes_accessed=6 * texts * WIDE,
    )(log_temp, bias, other, group_text, mine, in_hbm(coeffs))

    text_terms = lax.all_to_all(text_part, ("x", "y_lo"), 0, 0, tiled=True)
    got = swap_cores(give)
    blocks = lax.axis_size("z_hi")
    rows = blocks * ROWS
    split = WIDE // 2
    keep, left, right = call(
        fold,
        [(VMEM, shape((rows, WIDE), F32)), (VMEM, shape((rows, split), BF16)), (VMEM, shape((rows, WIDE - split), BF16))],
        [SMEM, VMEM, VMEM],
        bytes_accessed=16 * rows * WIDE,
    )(place_of("z_lo"), keep, got)
    left = lax.ppermute(left, COLUMN, [(i, i ^ 1) for i in range(column)])
    right = lax.ppermute(
        right, COLUMN, [(i, (i + (1 if i % 2 else -1)) % column) for i in range(column)]
    )
    (image_terms,) = call(
        last_fold,
        [(HBM, shape((blocks, ROWS, WIDE), BF16))],
        [VMEM, VMEM, VMEM],
        [pltpu.VMEM((blocks, ROWS, WIDE), BF16), pltpu.SemaphoreType.DMA((blocks,))],
        bytes_accessed=8 * rows * WIDE,
    )(keep, left, right)
    image_terms, text_terms = lax.optimization_barrier((image_terms, text_terms))
    text_terms = text_terms.reshape(near, far, ROWS, WIDTH)
    place = lax.axis_index("y_hi").astype(jnp.int32)
    text_keep, text_give = call(
        fold_text,
        [(VMEM, shape((far // 2, ROWS, WIDTH), F32)), (VMEM, shape((far // 2, ROWS, WIDTH), BF16))],
        [SMEM, VMEM],
        bytes_accessed=3 * texts * WIDTH,
    )((place % 2).reshape(1), text_terms)
    text_got = lax.ppermute(text_give, "y_hi", [(i, i ^ 1) for i in range(far)])
    text_keep, text_give = call(
        fold_text_again,
        [(VMEM, shape((ROWS, WIDTH), F32)), (VMEM, shape((ROWS, WIDTH), BF16))],
        [SMEM, VMEM, VMEM],
        bytes_accessed=10 * ROWS * WIDTH,
    )((place // 2).reshape(1), text_keep, text_got)
    text_got = lax.ppermute(text_give, "y_hi", [(i, i ^ 2) for i in range(far)])

    image_terms = lax.all_to_all(image_terms, "z_hi", 0, 0, tiled=True)

    (grad_text,) = call(
        finish_text,
        [(VMEM, shape((ROWS, WIDTH), F32))],
        [SMEM, VMEM, VMEM, VMEM],
        bytes_accessed=12 * ROWS * WIDTH,
    )(log_temp, text_embed, text_keep, text_got)
    grad_image, loss = call(
        functools.partial(finish_image, total),
        [(VMEM, shape((ROWS, WIDTH), F32)), (VMEM, shape((1, ROWS), F32))],
        [SMEM, VMEM, VMEM],
        bytes_accessed=2 * blocks * ROWS * WIDE,
    )(log_temp, image_embed, image_terms)
    return (grad_image, grad_text, loss.reshape(ROWS))


def solution(mesh):
    parts = Mesh(mesh.devices.reshape(4, 4, 2, 2, 8, 2), AXES)
    placed = (P(AXES, None), P(AXES, None), P(AXES), P(), P())
    return jax.shard_map(
        on_device,
        mesh=parts,
        in_specs=placed,
        out_specs=(P(AXES, None), P(AXES, None), P(AXES)),
        check_vma=False,
    )
```

```python
import functools

import jax
import jax.numpy as jnp
from jax import lax
from jax.experimental import pallas as pl
from jax.experimental.pallas import tpu as pltpu
from jax.sharding import Mesh, PartitionSpec as P

AXES = ("x", "y_hi", "core", "y_lo", "z_hi", "z_lo")
PLANE = ("x", "y_hi", "y_lo")
COLUMN = ("z_hi", "z_lo")
WIDTH = 1152
WIDE = WIDTH + 128
ROWS = 16
LABEL_BASE = 128
F32, BF16 = jnp.float32, jnp.bfloat16

VMEM = pl.BlockSpec(memory_space=pltpu.VMEM)
SMEM = pl.BlockSpec(memory_space=pltpu.SMEM)
HBM = pl.BlockSpec(memory_space=pltpu.HBM)


def call(kernel, outs, in_specs, scratch=(), flops=0, bytes_accessed=0, vmem=16):
    return pl.pallas_call(
        kernel,
        out_shape=[
            pltpu.HBM(shape.shape, shape.dtype) if spec is HBM else shape for spec, shape in outs
        ],
        in_specs=in_specs,
        out_specs=[spec for spec, _ in outs],
        scratch_shapes=list(scratch),
        compiler_params=pltpu.CompilerParams(vmem_limit_bytes=vmem * 1024 * 1024),
        cost_estimate=pl.CostEstimate(
            flops=flops, bytes_accessed=bytes_accessed, transcendentals=0
        ),
    )


def start(*copies):
    for copy in copies:
        copy.start()
    return copies


def wait(*copies):
    for copy in copies:
        copy.wait()


def unit_of(embed):
    values = embed.astype(F32)
    radius = jnp.sqrt(jnp.sum(values * values, axis=1, keepdims=True) + 1e-06)
    return values / radius, radius


def prepare(
    labels_ref, image_ref, text_ref, image_out, text_out, labels_now, image_now, text_now, text_wide, in_sem, out_sem
):
    labels_copy, image_copy, text_copy = start(
        pltpu.make_async_copy(labels_ref, labels_now, in_sem.at[0]),
        pltpu.make_async_copy(image_ref, image_now, in_sem.at[1]),
        pltpu.make_async_copy(text_ref, text_now, in_sem.at[2]),
    )
    wait(labels_copy)
    shape = (ROWS, 128)
    row = lax.broadcasted_iota(jnp.int32, shape, 0)
    lane = lax.broadcasted_iota(jnp.int32, shape, 1)
    label = jnp.zeros(shape, jnp.int32)
    for r in range(ROWS):
        label = jnp.where(row == r, labels_now[r], label)
    high, low = label >> 7, label & (LABEL_BASE - 1)
    norm = high * high + low * low
    norm_high, norm_low = norm >> 7, norm & (LABEL_BASE - 1)

    def features(values):
        out = jnp.zeros(shape, jnp.int32)
        for k, value in enumerate(values):
            out = jnp.where(lane == k, value, out)
        return out.astype(F32).astype(BF16)

    wait(text_copy)
    text_low = unit_of(text_now[...])[0].astype(BF16)
    marks = features((high, low, LABEL_BASE, 1, norm_high, norm_low))
    copies = text_wide.shape[0]
    for k in range(copies):
        text_wide[k, :, :WIDTH] = text_low
        text_wide[k, :, WIDTH:] = marks
    copies = start(
        *[
            pltpu.make_async_copy(text_wide, text_out.at[pl.ds(k * copies, copies)], out_sem.at[k])
            for k in range(text_out.shape[0] // copies)
        ]
    )
    wait(image_copy)
    image_out[:, :WIDTH] = unit_of(image_now[...])[0].astype(BF16)
    image_out[:, WIDTH:] = features((-2 * high, -2 * low, norm_high, norm_low, LABEL_BASE, 1))
    wait(*copies)


def dot(left, right, left_dim, right_dim):
    return lax.dot_general(
        left, right, (((left_dim,), (right_dim,)), ((), ())), preferred_element_type=F32
    )


def loss_pair(loss):
    lane = lax.broadcasted_iota(jnp.int32, (loss.shape[0], 128), 1)
    high = loss.astype(BF16).astype(F32)
    return jnp.where(lane == 0, high, jnp.where(lane == 1, loss - high, 0.0)).astype(BF16)


def half_tile(log_temp_ref, bias_ref, wide, text_wide):
    scale = jnp.exp(jnp.full((1, 1), log_temp_ref[0], F32))
    scores = scale * dot(wide[:, :WIDTH], text_wide[:, :WIDTH], 1, 1) + bias_ref[0]
    positive = dot(wide[:, WIDTH:], text_wide[:, WIDTH:], 1, 1) == 0.0
    small = jnp.exp(-jnp.abs(scores))
    losses = jnp.maximum(jnp.where(positive, -scores, scores), 0.0) + jnp.log1p(small)
    sigmoid = jnp.where(scores >= 0.0, 1.0, small) / (1.0 + small)
    coeffs = (sigmoid - jnp.where(positive, 1.0, 0.0)).astype(BF16)
    return jnp.sum(losses, axis=1, keepdims=True), coeffs


def first_tile(
    log_temp_ref, bias_ref, mine, text, coeffs_out, keep_out, coeffs_now, keep_now, out_sem
):
    loss, coeffs = half_tile(log_temp_ref, bias_ref, mine, text)
    coeffs_now[...] = coeffs
    (coeffs_copy,) = start(pltpu.make_async_copy(coeffs_now, coeffs_out, out_sem.at[0]))
    keep_now[:, :WIDTH] = dot(coeffs, text[:, :WIDTH], 1, 0)
    keep_now[:, WIDTH:] = loss_lane(loss)
    (keep_copy,) = start(pltpu.make_async_copy(keep_now, keep_out, out_sem.at[1]))
    wait(coeffs_copy, keep_copy)


def second_tile(
    order, log_temp_ref, bias_ref, other_ref, text_ref, mine_ref, coeffs_ref, give_out, text_out,
    other, text, mine, mine_coeffs, coeffs_now, give_now, text_now, in_sem, out_sem
):
    other_copy, text_copy, mine_copy, coeffs_copy = start(
        pltpu.make_async_copy(other_ref, other, in_sem.at[0]),
        pltpu.make_async_copy(text_ref, text, in_sem.at[1]),
        pltpu.make_async_copy(mine_ref, mine, in_sem.at[2]),
        pltpu.make_async_copy(coeffs_ref, mine_coeffs, in_sem.at[3]),
    )
    wait(other_copy, text_copy)
    loss, coeffs = half_tile(log_temp_ref, bias_ref, other, text)
    coeffs_now[...] = coeffs
    give_now[:, :WIDTH] = dot(coeffs, text[:, :WIDTH], 1, 0).astype(BF16)
    give_now[:, WIDTH:] = loss_pair(loss)
    copies = list(start(pltpu.make_async_copy(give_now, give_out, out_sem.at[0])))
    wait(mine_copy, coeffs_copy)
    chunk = 8
    for first in range(0, len(order), chunk):
        columns = pl.ds(first * ROWS, chunk * ROWS)
        total = dot(mine_coeffs[:, columns], mine[:, :WIDTH], 0, 0)
        total += dot(coeffs_now[:, columns], other[:, :WIDTH], 0, 0)
        for k in range(chunk):
            place = order[first + k]
            text_now[place] = total[k * ROWS : (k + 1) * ROWS].astype(BF16)
            copies += start(
                pltpu.make_async_copy(text_now.at[place], text_out.at[place], out_sem.at[1 + place])
            )
    wait(*copies)


def loss_lane(loss):
    lane = lax.broadcasted_iota(jnp.int32, (loss.shape[0], 128), 1)
    return jnp.where(lane == 0, loss, 0.0)


def fold(bit_ref, keep_ref, got_ref, keep_out, left_out, right_out):
    bit = bit_ref[0]
    split = left_out.shape[1]
    for pair in range(keep_out.shape[0] // ROWS):
        out = pl.ds(pair * ROWS, ROWS)
        for place in (bit, 1 - bit):
            rows = pl.ds((2 * pair + place) * ROWS, ROWS)
            terms = keep_ref[rows, :] + got_ref[rows, :].astype(F32)
            loss = jnp.sum(terms[:, WIDTH:], axis=1, keepdims=True)
            if place is bit:
                keep_out[out, :WIDTH] = terms[:, :WIDTH]
                keep_out[out, WIDTH:] = loss_lane(loss)
            else:
                left_out[out, :] = terms[:, :split].astype(BF16)
                right_out[out, : WIDTH - split] = terms[:, split:WIDTH].astype(BF16)
                right_out[out, WIDTH - split :] = loss_pair(loss)


def last_fold(keep_ref, left_ref, right_ref, part_out, out_ref, out_sem):
    copies = []
    split = left_ref.shape[1]
    for block in range(out_ref.shape[0]):
        rows = pl.ds(block * ROWS, ROWS)
        out_ref[block, :, :split] = (keep_ref[rows, :split] + left_ref[rows, :].astype(F32)).astype(BF16)
        terms = keep_ref[rows, split:] + right_ref[rows, :].astype(F32)
        out_ref[block, :, split:WIDTH] = terms[:, : WIDTH - split].astype(BF16)
        loss = jnp.sum(terms[:, WIDTH - split :], axis=1, keepdims=True)
        out_ref[block, :, WIDTH:] = loss_pair(loss)
        copies += start(
            pltpu.make_async_copy(out_ref.at[block], part_out.at[block], out_sem.at[block])
        )
    wait(*copies)


def unproject(log_temp_ref, embed_ref, terms):
    scale = jnp.exp(jnp.full((1, 1), log_temp_ref[0], F32))
    unit, radius = unit_of(embed_ref[...])
    grad = scale * terms
    return (grad - unit * jnp.sum(unit * grad, axis=1, keepdims=True)) / radius


def fold_text(bit_ref, terms_ref, keep_out, give_out):
    bit = bit_ref[0]
    for pair in range(keep_out.shape[0]):
        for out_ref, place in ((keep_out, bit), (give_out, 1 - bit)):
            terms = terms_ref[0, 2 * pair + place].astype(F32)
            for k in range(1, terms_ref.shape[0]):
                terms += terms_ref[k, 2 * pair + place].astype(F32)
            out_ref[pair] = terms.astype(out_ref.dtype)


def fold_text_again(bit_ref, keep_ref, got_ref, keep_out, give_out):
    bit = bit_ref[0]
    keep_out[...] = keep_ref[bit] + got_ref[bit].astype(F32)
    give_out[...] = (keep_ref[1 - bit] + got_ref[1 - bit].astype(F32)).astype(BF16)


def finish_text(log_temp_ref, embed_ref, keep_ref, got_ref, grad_out):
    terms = keep_ref[...] + got_ref[...].astype(F32)
    grad_out[...] = unproject(log_temp_ref, embed_ref, terms)


def finish_image(total, log_temp_ref, embed_ref, terms_ref, grad_out, loss_out):
    terms = terms_ref[0].astype(F32)
    for k in range(1, terms_ref.shape[0]):
        terms += terms_ref[k].astype(F32)
    grad_out[...] = unproject(log_temp_ref, embed_ref, terms[:, :WIDTH])
    loss = jnp.sum(terms[:, WIDTH:], axis=1, keepdims=True) / total
    row = lax.broadcasted_iota(jnp.int32, (ROWS, 128), 0)
    lane = lax.broadcasted_iota(jnp.int32, (ROWS, 128), 1)
    loss_out[...] = jnp.sum(jnp.where(row == lane, loss, 0.0), axis=0, keepdims=True)[:, :ROWS]


def in_hbm(array):
    return pltpu.with_memory_space_constraint(array, pltpu.HBM)


def place_of(axis):
    return lax.axis_index(axis).astype(jnp.int32).reshape(1)


def swap_cores(part):
    return lax.ppermute(part, "core", [(0, 1), (1, 0)])


def on_device(image_embed, text_embed, labels, log_temp, bias):
    total = ROWS * lax.axis_size(AXES)
    plane, column = lax.axis_size(PLANE), lax.axis_size(COLUMN)
    shape = jax.ShapeDtypeStruct

    image_wide, text_wide = call(
        prepare,
        [(VMEM, shape((ROWS, WIDE), BF16)), (HBM, shape((plane, ROWS, WIDE), BF16))],
        [HBM, HBM, HBM],
        [
            pltpu.SMEM((ROWS,), jnp.int32),
            pltpu.VMEM((ROWS, WIDTH), BF16),
            pltpu.VMEM((ROWS, WIDTH), BF16),
            pltpu.VMEM((8, ROWS, WIDE), BF16),
            pltpu.SemaphoreType.DMA((3,)),
            pltpu.SemaphoreType.DMA((plane // 8,)),
        ],
        bytes_accessed=plane * ROWS * WIDE * 2,
    )(in_hbm(labels), in_hbm(image_embed), in_hbm(text_embed))

    group_text = lax.all_to_all(text_wide, PLANE, 0, 0, tiled=True).reshape(-1, WIDE)
    mine = lax.all_gather(image_wide, COLUMN, axis=0, tiled=True)
    other = swap_cores(mine)

    half, texts = column * ROWS, plane * ROWS

    coeffs, keep = call(
        first_tile,
        [(HBM, shape((half, texts), BF16)), (HBM, shape((half, WIDE), F32))],
        [SMEM, SMEM, VMEM, VMEM],
        [
            pltpu.VMEM((half, texts), BF16),
            pltpu.VMEM((half, WIDE), F32),
            pltpu.SemaphoreType.DMA((2,)),
        ],
        flops=4 * half * texts * WIDTH,
        bytes_accessed=4 * texts * WIDE,
    )(log_temp, bias, mine, group_text)

    far, low = lax.axis_size("y_hi"), lax.axis_size("y_lo")
    near = plane // far
    order = [((b // low // far) * low + b % low) * far + (b // low) % far for b in range(plane)]
    give, text_part = call(
        functools.partial(second_tile, order),
        [(HBM, shape((half, WIDE), BF16)), (HBM, shape((plane, ROWS, WIDTH), BF16))],
        [SMEM, SMEM, HBM, HBM, HBM, HBM],
        [
            pltpu.VMEM((half, WIDE), BF16),
            pltpu.VMEM((texts, WIDE), BF16),
            pltpu.VMEM((half, WIDE), BF16),
            pltpu.VMEM((half, texts), BF16),
            pltpu.VMEM((half, texts), BF16),
            pltpu.VMEM((half, WIDE), BF16),
            pltpu.VMEM((plane, ROWS, WIDTH), BF16),
            pltpu.SemaphoreType.DMA((4,)),
            pltpu.SemaphoreType.DMA((plane + 1,)),
        ],
        flops=8 * half * texts * WIDTH,
        bytes_accessed=6 * texts * WIDE,
    )(log_temp, bias, other, group_text, mine, in_hbm(coeffs))

    text_terms = lax.all_to_all(text_part, ("x", "y_lo"), 0, 0, tiled=True)
    got = swap_cores(give)
    blocks = lax.axis_size("z_hi")
    rows = blocks * ROWS
    split = WIDE // 2
    keep, left, right = call(
        fold,
        [(VMEM, shape((rows, WIDE), F32)), (VMEM, shape((rows, split), BF16)), (VMEM, shape((rows, WIDE - split), BF16))],
        [SMEM, VMEM, VMEM],
        bytes_accessed=16 * rows * WIDE,
    )(place_of("z_lo"), keep, got)
    left = lax.ppermute(left, COLUMN, [(i, i ^ 1) for i in range(column)])
    right = lax.ppermute(
        right, COLUMN, [(i, (i + (1 if i % 2 else -1)) % column) for i in range(column)]
    )
    (image_terms,) = call(
        last_fold,
        [(HBM, shape((blocks, ROWS, WIDE), BF16))],
        [VMEM, VMEM, VMEM],
        [pltpu.VMEM((blocks, ROWS, WIDE), BF16), pltpu.SemaphoreType.DMA((blocks,))],
        bytes_accessed=8 * rows * WIDE,
    )(keep, left, right)
    image_terms, text_terms = lax.optimization_barrier((image_terms, text_terms))
    text_terms = text_terms.reshape(near, far, ROWS, WIDTH)
    place = lax.axis_index("y_hi").astype(jnp.int32)
    text_keep, text_give = call(
        fold_text,
        [(VMEM, shape((far // 2, ROWS, WIDTH), F32)), (VMEM, shape((far // 2, ROWS, WIDTH), BF16))],
        [SMEM, VMEM],
        bytes_accessed=3 * texts * WIDTH,
    )((place % 2).reshape(1), text_terms)
    text_got = lax.ppermute(text_give, "y_hi", [(i, i ^ 1) for i in range(far)])
    text_keep, text_give = call(
        fold_text_again,
        [(VMEM, shape((ROWS, WIDTH), F32)), (VMEM, shape((ROWS, WIDTH), BF16))],
        [SMEM, VMEM, VMEM],
        bytes_accessed=10 * ROWS * WIDTH,
    )((place // 2).reshape(1), text_keep, text_got)
    text_got = lax.ppermute(text_give, "y_hi", [(i, i ^ 2) for i in range(far)])

    image_terms = lax.all_to_all(image_terms, "z_hi", 0, 0, tiled=True)

    (grad_text,) = call(
        finish_text,
        [(VMEM, shape((ROWS, WIDTH), F32))],
        [SMEM, VMEM, VMEM, VMEM],
        bytes_accessed=12 * ROWS * WIDTH,
    )(log_temp, text_embed, text_keep, text_got)
    grad_image, loss = call(
        functools.partial(finish_image, total),
        [(VMEM, shape((ROWS, WIDTH), F32)), (VMEM, shape((1, ROWS), F32))],
        [SMEM, VMEM, VMEM],
        bytes_accessed=2 * blocks * ROWS * WIDE,
    )(log_temp, image_embed, image_terms)
    return (grad_image, grad_text, loss.reshape(ROWS))


def solution(mesh):
    parts = Mesh(mesh.devices.reshape(4, 4, 2, 2, 8, 2), AXES)
    placed = (P(AXES, None), P(AXES, None), P(AXES), P(), P())
    return jax.shard_map(
        on_device,
        mesh=parts,
        in_specs=placed,
        out_specs=(P(AXES, None), P(AXES, None), P(AXES)),
        check_vma=False,
    )
```

```python
import functools

import jax
import jax.numpy as jnp
from jax import lax
from jax.experimental import pallas as pl
from jax.experimental.pallas import tpu as pltpu
from jax.sharding import Mesh, PartitionSpec as P

AXES = ("x", "y_hi", "core", "y_lo", "z_hi", "z_lo")
PLANE = ("x", "y_hi", "y_lo")
COLUMN = ("z_hi", "z_lo")
WIDTH = 1152
WIDE = WIDTH + 128
ROWS = 16
LABEL_BASE = 128
F32, BF16 = jnp.float32, jnp.bfloat16

VMEM = pl.BlockSpec(memory_space=pltpu.VMEM)
SMEM = pl.BlockSpec(memory_space=pltpu.SMEM)
HBM = pl.BlockSpec(memory_space=pltpu.HBM)


def call(kernel, outs, in_specs, scratch=(), flops=0, bytes_accessed=0, vmem=16):
    return pl.pallas_call(
        kernel,
        out_shape=[
            pltpu.HBM(shape.shape, shape.dtype) if spec is HBM else shape for spec, shape in outs
        ],
        in_specs=in_specs,
        out_specs=[spec for spec, _ in outs],
        scratch_shapes=list(scratch),
        compiler_params=pltpu.CompilerParams(vmem_limit_bytes=vmem * 1024 * 1024),
        cost_estimate=pl.CostEstimate(
            flops=flops, bytes_accessed=bytes_accessed, transcendentals=0
        ),
    )


def start(*copies):
    for copy in copies:
        copy.start()
    return copies


def wait(*copies):
    for copy in copies:
        copy.wait()


def unit_of(embed):
    values = embed.astype(F32)
    radius = jnp.sqrt(jnp.sum(values * values, axis=1, keepdims=True) + 1e-06)
    return values / radius, radius


def prepare(
    labels_ref, image_ref, text_ref, image_out, text_out, labels_now, image_now, text_now, text_wide, in_sem, out_sem
):
    labels_copy, image_copy, text_copy = start(
        pltpu.make_async_copy(labels_ref, labels_now, in_sem.at[0]),
        pltpu.make_async_copy(image_ref, image_now, in_sem.at[1]),
        pltpu.make_async_copy(text_ref, text_now, in_sem.at[2]),
    )
    wait(labels_copy)
    shape = (ROWS, 128)
    row = lax.broadcasted_iota(jnp.int32, shape, 0)
    lane = lax.broadcasted_iota(jnp.int32, shape, 1)
    label = jnp.zeros(shape, jnp.int32)
    for r in range(ROWS):
        label = jnp.where(row == r, labels_now[r], label)
    high, low = label >> 7, label & (LABEL_BASE - 1)
    norm = high * high + low * low
    norm_high, norm_low = norm >> 7, norm & (LABEL_BASE - 1)

    def features(values):
        out = jnp.zeros(shape, jnp.int32)
        for k, value in enumerate(values):
            out = jnp.where(lane == k, value, out)
        return out.astype(F32).astype(BF16)

    wait(text_copy)
    text_low = unit_of(text_now[...])[0].astype(BF16)
    marks = features((high, low, LABEL_BASE, 1, norm_high, norm_low))
    copies = text_wide.shape[0]
    for k in range(copies):
        text_wide[k, :, :WIDTH] = text_low
        text_wide[k, :, WIDTH:] = marks
    copies = start(
        *[
            pltpu.make_async_copy(text_wide, text_out.at[pl.ds(k * copies, copies)], out_sem.at[k])
            for k in range(text_out.shape[0] // copies)
        ]
    )
    wait(image_copy)
    image_out[:, :WIDTH] = unit_of(image_now[...])[0].astype(BF16)
    image_out[:, WIDTH:] = features((-2 * high, -2 * low, norm_high, norm_low, LABEL_BASE, 1))
    wait(*copies)


def dot(left, right, left_dim, right_dim):
    return lax.dot_general(
        left, right, (((left_dim,), (right_dim,)), ((), ())), preferred_element_type=F32
    )


def loss_pair(loss):
    lane = lax.broadcasted_iota(jnp.int32, (loss.shape[0], 128), 1)
    high = loss.astype(BF16).astype(F32)
    return jnp.where(lane == 0, high, jnp.where(lane == 1, loss - high, 0.0)).astype(BF16)


def half_tile(log_temp_ref, bias_ref, wide, text_wide):
    scale = jnp.exp(jnp.full((1, 1), log_temp_ref[0], F32))
    scores = scale * dot(wide[:, :WIDTH], text_wide[:, :WIDTH], 1, 1) + bias_ref[0]
    positive = dot(wide[:, WIDTH:], text_wide[:, WIDTH:], 1, 1) == 0.0
    small = jnp.exp(-jnp.abs(scores))
    losses = jnp.maximum(jnp.where(positive, -scores, scores), 0.0) + jnp.log1p(small)
    sigmoid = jnp.where(scores >= 0.0, 1.0, small) / (1.0 + small)
    coeffs = (sigmoid - jnp.where(positive, 1.0, 0.0)).astype(BF16)
    return jnp.sum(losses, axis=1, keepdims=True), coeffs


def first_tile(
    log_temp_ref, bias_ref, mine, text, coeffs_out, keep_out, coeffs_now, keep_now, out_sem
):
    loss, coeffs = half_tile(log_temp_ref, bias_ref, mine, text)
    coeffs_now[...] = coeffs
    (coeffs_copy,) = start(pltpu.make_async_copy(coeffs_now, coeffs_out, out_sem.at[0]))
    keep_now[:, :WIDTH] = dot(coeffs, text[:, :WIDTH], 1, 0)
    keep_now[:, WIDTH:] = loss_lane(loss)
    (keep_copy,) = start(pltpu.make_async_copy(keep_now, keep_out, out_sem.at[1]))
    wait(coeffs_copy, keep_copy)


def second_tile(
    order, log_temp_ref, bias_ref, other_ref, text_ref, mine_ref, coeffs_ref, give_out, text_out,
    other, text, mine, mine_coeffs, coeffs_now, give_now, text_now, in_sem, out_sem
):
    other_copy, text_copy, mine_copy, coeffs_copy = start(
        pltpu.make_async_copy(other_ref, other, in_sem.at[0]),
        pltpu.make_async_copy(text_ref, text, in_sem.at[1]),
        pltpu.make_async_copy(mine_ref, mine, in_sem.at[2]),
        pltpu.make_async_copy(coeffs_ref, mine_coeffs, in_sem.at[3]),
    )
    wait(other_copy, text_copy)
    loss, coeffs = half_tile(log_temp_ref, bias_ref, other, text)
    coeffs_now[...] = coeffs
    give_now[:, :WIDTH] = dot(coeffs, text[:, :WIDTH], 1, 0).astype(BF16)
    give_now[:, WIDTH:] = loss_pair(loss)
    copies = list(start(pltpu.make_async_copy(give_now, give_out, out_sem.at[0])))
    wait(mine_copy, coeffs_copy)
    chunk = 8
    for first in range(0, len(order), chunk):
        columns = pl.ds(first * ROWS, chunk * ROWS)
        total = dot(mine_coeffs[:, columns], mine[:, :WIDTH], 0, 0)
        total += dot(coeffs_now[:, columns], other[:, :WIDTH], 0, 0)
        for k in range(chunk):
            place = order[first + k]
            text_now[place] = total[k * ROWS : (k + 1) * ROWS].astype(BF16)
            copies += start(
                pltpu.make_async_copy(text_now.at[place], text_out.at[place], out_sem.at[1 + place])
            )
    wait(*copies)


def loss_lane(loss):
    lane = lax.broadcasted_iota(jnp.int32, (loss.shape[0], 128), 1)
    return jnp.where(lane == 0, loss, 0.0)


def fold(bit_ref, keep_ref, got_ref, keep_out, left_out, right_out):
    bit = bit_ref[0]
    split = left_out.shape[1]
    for pair in range(keep_out.shape[0] // ROWS):
        out = pl.ds(pair * ROWS, ROWS)
        for place in (bit, 1 - bit):
            rows = pl.ds((2 * pair + place) * ROWS, ROWS)
            terms = keep_ref[rows, :] + got_ref[rows, :].astype(F32)
            loss = jnp.sum(terms[:, WIDTH:], axis=1, keepdims=True)
            if place is bit:
                keep_out[out, :WIDTH] = terms[:, :WIDTH]
                keep_out[out, WIDTH:] = loss_lane(loss)
            else:
                left_out[out, :] = terms[:, :split].astype(BF16)
                right_out[out, : WIDTH - split] = terms[:, split:WIDTH].astype(BF16)
                right_out[out, WIDTH - split :] = loss_pair(loss)


def last_fold(keep_ref, left_ref, right_ref, part_out, out_ref, out_sem):
    copies = []
    split = left_ref.shape[1]
    for block in range(out_ref.shape[0]):
        rows = pl.ds(block * ROWS, ROWS)
        out_ref[block, :, :split] = (keep_ref[rows, :split] + left_ref[rows, :].astype(F32)).astype(BF16)
        terms = keep_ref[rows, split:] + right_ref[rows, :].astype(F32)
        out_ref[block, :, split:WIDTH] = terms[:, : WIDTH - split].astype(BF16)
        loss = jnp.sum(terms[:, WIDTH - split :], axis=1, keepdims=True)
        out_ref[block, :, WIDTH:] = loss_pair(loss)
        copies += start(
            pltpu.make_async_copy(out_ref.at[block], part_out.at[block], out_sem.at[block])
        )
    wait(*copies)


def unproject(log_temp_ref, embed_ref, terms):
    scale = jnp.exp(jnp.full((1, 1), log_temp_ref[0], F32))
    unit, radius = unit_of(embed_ref[...])
    grad = scale * terms
    return (grad - unit * jnp.sum(unit * grad, axis=1, keepdims=True)) / radius


def fold_text(bit_ref, terms_ref, keep_out, give_out):
    bit = bit_ref[0]
    for pair in range(keep_out.shape[0]):
        for out_ref, place in ((keep_out, bit), (give_out, 1 - bit)):
            terms = terms_ref[0, 2 * pair + place].astype(F32)
            for k in range(1, terms_ref.shape[0]):
                terms += terms_ref[k, 2 * pair + place].astype(F32)
            out_ref[pair] = terms.astype(out_ref.dtype)


def fold_text_again(bit_ref, keep_ref, got_ref, keep_out, give_out):
    bit = bit_ref[0]
    keep_out[...] = keep_ref[bit] + got_ref[bit].astype(F32)
    give_out[...] = (keep_ref[1 - bit] + got_ref[1 - bit].astype(F32)).astype(BF16)


def finish_text(log_temp_ref, embed_ref, keep_ref, got_ref, grad_out):
    terms = keep_ref[...] + got_ref[...].astype(F32)
    grad_out[...] = unproject(log_temp_ref, embed_ref, terms)


def finish_image(total, log_temp_ref, embed_ref, terms_ref, grad_out, loss_out):
    terms = terms_ref[0].astype(F32)
    for k in range(1, terms_ref.shape[0]):
        terms += terms_ref[k].astype(F32)
    grad_out[...] = unproject(log_temp_ref, embed_ref, terms[:, :WIDTH])
    loss = jnp.sum(terms[:, WIDTH:], axis=1, keepdims=True) / total
    row = lax.broadcasted_iota(jnp.int32, (ROWS, 128), 0)
    lane = lax.broadcasted_iota(jnp.int32, (ROWS, 128), 1)
    loss_out[...] = jnp.sum(jnp.where(row == lane, loss, 0.0), axis=0, keepdims=True)[:, :ROWS]


def in_hbm(array):
    return pltpu.with_memory_space_constraint(array, pltpu.HBM)


def place_of(axis):
    return lax.axis_index(axis).astype(jnp.int32).reshape(1)


def swap_cores(part):
    return lax.ppermute(part, "core", [(0, 1), (1, 0)])


def on_device(image_embed, text_embed, labels, log_temp, bias):
    total = ROWS * lax.axis_size(AXES)
    plane, column = lax.axis_size(PLANE), lax.axis_size(COLUMN)
    shape = jax.ShapeDtypeStruct

    image_wide, text_wide = call(
        prepare,
        [(VMEM, shape((ROWS, WIDE), BF16)), (HBM, shape((plane, ROWS, WIDE), BF16))],
        [HBM, HBM, HBM],
        [
            pltpu.SMEM((ROWS,), jnp.int32),
            pltpu.VMEM((ROWS, WIDTH), BF16),
            pltpu.VMEM((ROWS, WIDTH), BF16),
            pltpu.VMEM((8, ROWS, WIDE), BF16),
            pltpu.SemaphoreType.DMA((3,)),
            pltpu.SemaphoreType.DMA((plane // 8,)),
        ],
        bytes_accessed=plane * ROWS * WIDE * 2,
    )(in_hbm(labels), in_hbm(image_embed), in_hbm(text_embed))

    group_text = lax.all_to_all(text_wide, PLANE, 0, 0, tiled=True).reshape(-1, WIDE)
    mine = lax.all_gather(image_wide, COLUMN, axis=0, tiled=True)
    other = swap_cores(mine)

    half, texts = column * ROWS, plane * ROWS

    coeffs, keep = call(
        first_tile,
        [(HBM, shape((half, texts), BF16)), (HBM, shape((half, WIDE), F32))],
        [SMEM, SMEM, VMEM, VMEM],
        [
            pltpu.VMEM((half, texts), BF16),
            pltpu.VMEM((half, WIDE), F32),
            pltpu.SemaphoreType.DMA((2,)),
        ],
        flops=4 * half * texts * WIDTH,
        bytes_accessed=4 * texts * WIDE,
    )(log_temp, bias, mine, group_text)

    far, low = lax.axis_size("y_hi"), lax.axis_size("y_lo")
    near = plane // far
    wide = plane // far // low
    order = [((b % low) * wide + b // low // far) * far + (b // low) % far for b in range(plane)]
    give, text_part = call(
        functools.partial(second_tile, order),
        [(HBM, shape((half, WIDE), BF16)), (HBM, shape((plane, ROWS, WIDTH), BF16))],
        [SMEM, SMEM, HBM, HBM, HBM, HBM],
        [
            pltpu.VMEM((half, WIDE), BF16),
            pltpu.VMEM((texts, WIDE), BF16),
            pltpu.VMEM((half, WIDE), BF16),
            pltpu.VMEM((half, texts), BF16),
            pltpu.VMEM((half, texts), BF16),
            pltpu.VMEM((half, WIDE), BF16),
            pltpu.VMEM((plane, ROWS, WIDTH), BF16),
            pltpu.SemaphoreType.DMA((4,)),
            pltpu.SemaphoreType.DMA((plane + 1,)),
        ],
        flops=8 * half * texts * WIDTH,
        bytes_accessed=6 * texts * WIDE,
    )(log_temp, bias, other, group_text, mine, in_hbm(coeffs))

    text_terms = lax.all_to_all(text_part, ("y_lo", "x"), 0, 0, tiled=True)
    got = swap_cores(give)
    blocks = lax.axis_size("z_hi")
    rows = blocks * ROWS
    split = WIDE // 2
    keep, left, right = call(
        fold,
        [(VMEM, shape((rows, WIDE), F32)), (VMEM, shape((rows, split), BF16)), (VMEM, shape((rows, WIDE - split), BF16))],
        [SMEM, VMEM, VMEM],
        bytes_accessed=16 * rows * WIDE,
    )(place_of("z_lo"), keep, got)
    left = lax.ppermute(left, COLUMN, [(i, i ^ 1) for i in range(column)])
    right = lax.ppermute(
        right, COLUMN, [(i, (i + (1 if i % 2 else -1)) % column) for i in range(column)]
    )
    (image_terms,) = call(
        last_fold,
        [(HBM, shape((blocks, ROWS, WIDE), BF16))],
        [VMEM, VMEM, VMEM],
        [pltpu.VMEM((blocks, ROWS, WIDE), BF16), pltpu.SemaphoreType.DMA((blocks,))],
        bytes_accessed=8 * rows * WIDE,
    )(keep, left, right)
    image_terms, text_terms = lax.optimization_barrier((image_terms, text_terms))
    text_terms = text_terms.reshape(near, far, ROWS, WIDTH)
    place = lax.axis_index("y_hi").astype(jnp.int32)
    text_keep, text_give = call(
        fold_text,
        [(VMEM, shape((far // 2, ROWS, WIDTH), F32)), (VMEM, shape((far // 2, ROWS, WIDTH), BF16))],
        [SMEM, VMEM],
        bytes_accessed=3 * texts * WIDTH,
    )((place % 2).reshape(1), text_terms)
    text_got = lax.ppermute(text_give, "y_hi", [(i, i ^ 1) for i in range(far)])
    text_keep, text_give = call(
        fold_text_again,
        [(VMEM, shape((ROWS, WIDTH), F32)), (VMEM, shape((ROWS, WIDTH), BF16))],
        [SMEM, VMEM, VMEM],
        bytes_accessed=10 * ROWS * WIDTH,
    )((place // 2).reshape(1), text_keep, text_got)
    text_got = lax.ppermute(text_give, "y_hi", [(i, i ^ 2) for i in range(far)])

    image_terms = lax.all_to_all(image_terms, "z_hi", 0, 0, tiled=True)

    (grad_text,) = call(
        finish_text,
        [(VMEM, shape((ROWS, WIDTH), F32))],
        [SMEM, VMEM, VMEM, VMEM],
        bytes_accessed=12 * ROWS * WIDTH,
    )(log_temp, text_embed, text_keep, text_got)
    grad_image, loss = call(
        functools.partial(finish_image, total),
        [(VMEM, shape((ROWS, WIDTH), F32)), (VMEM, shape((1, ROWS), F32))],
        [SMEM, VMEM, VMEM],
        bytes_accessed=2 * blocks * ROWS * WIDE,
    )(log_temp, image_embed, image_terms)
    return (grad_image, grad_text, loss.reshape(ROWS))


def solution(mesh):
    parts = Mesh(mesh.devices.reshape(4, 4, 2, 2, 8, 2), AXES)
    placed = (P(AXES, None), P(AXES, None), P(AXES), P(), P())
    return jax.shard_map(
        on_device,
        mesh=parts,
        in_specs=placed,
        out_specs=(P(AXES, None), P(AXES, None), P(AXES)),
        check_vma=False,
    )
```

```python
import functools

import jax
import jax.numpy as jnp
from jax import lax
from jax.experimental import pallas as pl
from jax.experimental.pallas import tpu as pltpu
from jax.sharding import Mesh, PartitionSpec as P

AXES = ("x", "y_hi", "core", "y_lo", "z_hi", "z_lo")
PLANE = ("x", "y_hi", "y_lo")
COLUMN = ("z_hi", "z_lo")
WIDTH = 1152
WIDE = WIDTH + 128
ROWS = 16
LABEL_BASE = 128
F32, BF16 = jnp.float32, jnp.bfloat16

VMEM = pl.BlockSpec(memory_space=pltpu.VMEM)
SMEM = pl.BlockSpec(memory_space=pltpu.SMEM)
HBM = pl.BlockSpec(memory_space=pltpu.HBM)


def call(kernel, outs, in_specs, scratch=(), flops=0, bytes_accessed=0, vmem=16):
    return pl.pallas_call(
        kernel,
        out_shape=[
            pltpu.HBM(shape.shape, shape.dtype) if spec is HBM else shape for spec, shape in outs
        ],
        in_specs=in_specs,
        out_specs=[spec for spec, _ in outs],
        scratch_shapes=list(scratch),
        compiler_params=pltpu.CompilerParams(vmem_limit_bytes=vmem * 1024 * 1024),
        cost_estimate=pl.CostEstimate(
            flops=flops, bytes_accessed=bytes_accessed, transcendentals=0
        ),
    )


def start(*copies):
    for copy in copies:
        copy.start()
    return copies


def wait(*copies):
    for copy in copies:
        copy.wait()


def unit_of(embed):
    values = embed.astype(F32)
    radius = jnp.sqrt(jnp.sum(values * values, axis=1, keepdims=True) + 1e-06)
    return values / radius, radius


def prepare(
    labels_ref, image_ref, text_ref, image_out, text_out, labels_now, image_now, text_now, text_wide, in_sem, out_sem
):
    labels_copy, image_copy, text_copy = start(
        pltpu.make_async_copy(labels_ref, labels_now, in_sem.at[0]),
        pltpu.make_async_copy(image_ref, image_now, in_sem.at[1]),
        pltpu.make_async_copy(text_ref, text_now, in_sem.at[2]),
    )
    wait(labels_copy)
    shape = (ROWS, 128)
    row = lax.broadcasted_iota(jnp.int32, shape, 0)
    lane = lax.broadcasted_iota(jnp.int32, shape, 1)
    label = jnp.zeros(shape, jnp.int32)
    for r in range(ROWS):
        label = jnp.where(row == r, labels_now[r], label)
    high, low = label >> 7, label & (LABEL_BASE - 1)
    norm = high * high + low * low
    norm_high, norm_low = norm >> 7, norm & (LABEL_BASE - 1)

    def features(values):
        out = jnp.zeros(shape, jnp.int32)
        for k, value in enumerate(values):
            out = jnp.where(lane == k, value, out)
        return out.astype(F32).astype(BF16)

    wait(text_copy)
    text_low = unit_of(text_now[...])[0].astype(BF16)
    marks = features((high, low, LABEL_BASE, 1, norm_high, norm_low))
    copies = text_wide.shape[0]
    for k in range(copies):
        text_wide[k, :, :WIDTH] = text_low
        text_wide[k, :, WIDTH:] = marks
    copies = start(
        *[
            pltpu.make_async_copy(text_wide, text_out.at[pl.ds(k * copies, copies)], out_sem.at[k])
            for k in range(text_out.shape[0] // copies)
        ]
    )
    wait(image_copy)
    image_out[:, :WIDTH] = unit_of(image_now[...])[0].astype(BF16)
    image_out[:, WIDTH:] = features((-2 * high, -2 * low, norm_high, norm_low, LABEL_BASE, 1))
    wait(*copies)


def dot(left, right, left_dim, right_dim):
    return lax.dot_general(
        left, right, (((left_dim,), (right_dim,)), ((), ())), preferred_element_type=F32
    )


def loss_pair(loss):
    lane = lax.broadcasted_iota(jnp.int32, (loss.shape[0], 128), 1)
    high = loss.astype(BF16).astype(F32)
    return jnp.where(lane == 0, high, jnp.where(lane == 1, loss - high, 0.0)).astype(BF16)


def half_tile(log_temp_ref, bias_ref, wide, text_wide):
    scale = jnp.exp(jnp.full((1, 1), log_temp_ref[0], F32))
    scores = scale * dot(wide[:, :WIDTH], text_wide[:, :WIDTH], 1, 1) + bias_ref[0]
    positive = dot(wide[:, WIDTH:], text_wide[:, WIDTH:], 1, 1) == 0.0
    small = jnp.exp(-jnp.abs(scores))
    losses = jnp.maximum(jnp.where(positive, -scores, scores), 0.0) + jnp.log(1.0 + small)
    sigmoid = jnp.where(scores >= 0.0, 1.0, small) / (1.0 + small)
    coeffs = (sigmoid - jnp.where(positive, 1.0, 0.0)).astype(BF16)
    return jnp.sum(losses, axis=1, keepdims=True), coeffs


def first_tile(
    log_temp_ref, bias_ref, mine, text, coeffs_out, keep_out, coeffs_now, keep_now, out_sem
):
    loss, coeffs = half_tile(log_temp_ref, bias_ref, mine, text)
    coeffs_now[...] = coeffs
    (coeffs_copy,) = start(pltpu.make_async_copy(coeffs_now, coeffs_out, out_sem.at[0]))
    keep_now[:, :WIDTH] = dot(coeffs, text[:, :WIDTH], 1, 0)
    keep_now[:, WIDTH:] = loss_lane(loss)
    (keep_copy,) = start(pltpu.make_async_copy(keep_now, keep_out, out_sem.at[1]))
    wait(coeffs_copy, keep_copy)


def second_tile(
    order, far, log_temp_ref, bias_ref, other_ref, text_ref, mine_ref, coeffs_ref, give_out, text_out,
    other, text, mine, mine_coeffs, coeffs_now, give_now, text_now, in_sem, out_sem
):
    other_copy, text_copy, mine_copy, coeffs_copy = start(
        pltpu.make_async_copy(other_ref, other, in_sem.at[0]),
        pltpu.make_async_copy(text_ref, text, in_sem.at[1]),
        pltpu.make_async_copy(mine_ref, mine, in_sem.at[2]),
        pltpu.make_async_copy(coeffs_ref, mine_coeffs, in_sem.at[3]),
    )
    wait(other_copy, text_copy)
    loss, coeffs = half_tile(log_temp_ref, bias_ref, other, text)
    coeffs_now[...] = coeffs
    give_now[:, :WIDTH] = dot(coeffs, text[:, :WIDTH], 1, 0).astype(BF16)
    give_now[:, WIDTH:] = loss_pair(loss)
    copies = list(start(pltpu.make_async_copy(give_now, give_out, out_sem.at[0])))
    wait(mine_copy, coeffs_copy)
    chunk = 8
    for first in range(0, len(order), chunk):
        columns = pl.ds(first * ROWS, chunk * ROWS)
        total = dot(mine_coeffs[:, columns], mine[:, :WIDTH], 0, 0)
        total += dot(coeffs_now[:, columns], other[:, :WIDTH], 0, 0)
        for k in range(chunk):
            text_now[order[first + k]] = total[k * ROWS : (k + 1) * ROWS].astype(BF16)
        places = sorted(order[first : first + chunk])
        for run in range(0, chunk, far):
            blocks = pl.ds(places[run], far)
            copies += start(
                pltpu.make_async_copy(text_now.at[blocks], text_out.at[blocks], out_sem.at[len(copies)])
            )
    wait(*copies)


def loss_lane(loss):
    lane = lax.broadcasted_iota(jnp.int32, (loss.shape[0], 128), 1)
    return jnp.where(lane == 0, loss, 0.0)


def fold(bit_ref, keep_ref, got_ref, keep_out, left_out, right_out):
    bit = bit_ref[0]
    split = left_out.shape[1]
    for pair in range(keep_out.shape[0] // ROWS):
        out = pl.ds(pair * ROWS, ROWS)
        for place in (bit, 1 - bit):
            rows = pl.ds((2 * pair + place) * ROWS, ROWS)
            terms = keep_ref[rows, :] + got_ref[rows, :].astype(F32)
            loss = jnp.sum(terms[:, WIDTH:], axis=1, keepdims=True)
            if place is bit:
                keep_out[out, :WIDTH] = terms[:, :WIDTH]
                keep_out[out, WIDTH:] = loss_lane(loss)
            else:
                left_out[out, :] = terms[:, :split].astype(BF16)
                right_out[out, : WIDTH - split] = terms[:, split:WIDTH].astype(BF16)
                right_out[out, WIDTH - split :] = loss_pair(loss)


def last_fold(keep_ref, left_ref, right_ref, part_out, out_ref, out_sem):
    copies = []
    split = left_ref.shape[1]
    for block in range(out_ref.shape[0]):
        rows = pl.ds(block * ROWS, ROWS)
        out_ref[block, :, :split] = (keep_ref[rows, :split] + left_ref[rows, :].astype(F32)).astype(BF16)
        terms = keep_ref[rows, split:] + right_ref[rows, :].astype(F32)
        out_ref[block, :, split:WIDTH] = terms[:, : WIDTH - split].astype(BF16)
        loss = jnp.sum(terms[:, WIDTH - split :], axis=1, keepdims=True)
        out_ref[block, :, WIDTH:] = loss_pair(loss)
        copies += start(
            pltpu.make_async_copy(out_ref.at[block], part_out.at[block], out_sem.at[block])
        )
    wait(*copies)


def unproject(log_temp_ref, embed_ref, terms):
    scale = jnp.exp(jnp.full((1, 1), log_temp_ref[0], F32))
    unit, radius = unit_of(embed_ref[...])
    grad = scale * terms
    return (grad - unit * jnp.sum(unit * grad, axis=1, keepdims=True)) / radius


def fold_text(bit_ref, terms_ref, keep_out, give_out):
    bit = bit_ref[0]
    for pair in range(keep_out.shape[0]):
        for out_ref, place in ((keep_out, bit), (give_out, 1 - bit)):
            terms = terms_ref[0, 2 * pair + place].astype(F32)
            for k in range(1, terms_ref.shape[0]):
                terms += terms_ref[k, 2 * pair + place].astype(F32)
            out_ref[pair] = terms.astype(out_ref.dtype)


def fold_text_again(bit_ref, keep_ref, got_ref, keep_out, give_out):
    bit = bit_ref[0]
    keep_out[...] = keep_ref[bit] + got_ref[bit].astype(F32)
    give_out[...] = (keep_ref[1 - bit] + got_ref[1 - bit].astype(F32)).astype(BF16)


def finish_text(log_temp_ref, embed_ref, keep_ref, got_ref, grad_out):
    terms = keep_ref[...] + got_ref[...].astype(F32)
    grad_out[...] = unproject(log_temp_ref, embed_ref, terms)


def finish_image(total, log_temp_ref, embed_ref, terms_ref, grad_out, loss_out):
    terms = terms_ref[0].astype(F32)
    for k in range(1, terms_ref.shape[0]):
        terms += terms_ref[k].astype(F32)
    grad_out[...] = unproject(log_temp_ref, embed_ref, terms[:, :WIDTH])
    loss = jnp.sum(terms[:, WIDTH:], axis=1, keepdims=True) / total
    row = lax.broadcasted_iota(jnp.int32, (ROWS, 128), 0)
    lane = lax.broadcasted_iota(jnp.int32, (ROWS, 128), 1)
    loss_out[...] = jnp.sum(jnp.where(row == lane, loss, 0.0), axis=0, keepdims=True)[:, :ROWS]


def in_hbm(array):
    return pltpu.with_memory_space_constraint(array, pltpu.HBM)


def place_of(axis):
    return lax.axis_index(axis).astype(jnp.int32).reshape(1)


def swap_cores(part):
    return lax.ppermute(part, "core", [(0, 1), (1, 0)])


def on_device(image_embed, text_embed, labels, log_temp, bias):
    total = ROWS * lax.axis_size(AXES)
    plane, column = lax.axis_size(PLANE), lax.axis_size(COLUMN)
    shape = jax.ShapeDtypeStruct

    image_wide, text_wide = call(
        prepare,
        [(VMEM, shape((ROWS, WIDE), BF16)), (HBM, shape((plane, ROWS, WIDE), BF16))],
        [HBM, HBM, HBM],
        [
            pltpu.SMEM((ROWS,), jnp.int32),
            pltpu.VMEM((ROWS, WIDTH), BF16),
            pltpu.VMEM((ROWS, WIDTH), BF16),
            pltpu.VMEM((8, ROWS, WIDE), BF16),
            pltpu.SemaphoreType.DMA((3,)),
            pltpu.SemaphoreType.DMA((plane // 8,)),
        ],
        bytes_accessed=plane * ROWS * WIDE * 2,
    )(in_hbm(labels), in_hbm(image_embed), in_hbm(text_embed))

    group_text = lax.all_to_all(text_wide, PLANE, 0, 0, tiled=True).reshape(-1, WIDE)
    mine = lax.all_gather(image_wide, COLUMN, axis=0, tiled=True)
    other = swap_cores(mine)

    half, texts = column * ROWS, plane * ROWS

    coeffs, keep = call(
        first_tile,
        [(HBM, shape((half, texts), BF16)), (HBM, shape((half, WIDE), F32))],
        [SMEM, SMEM, VMEM, VMEM],
        [
            pltpu.VMEM((half, texts), BF16),
            pltpu.VMEM((half, WIDE), F32),
            pltpu.SemaphoreType.DMA((2,)),
        ],
        flops=4 * half * texts * WIDTH,
        bytes_accessed=4 * texts * WIDE,
    )(log_temp, bias, mine, group_text)

    far, low = lax.axis_size("y_hi"), lax.axis_size("y_lo")
    near = plane // far
    wide = plane // far // low
    order = [((b % low) * wide + b // low // far) * far + (b // low) % far for b in range(plane)]
    give, text_part = call(
        functools.partial(second_tile, order, far),
        [(HBM, shape((half, WIDE), BF16)), (HBM, shape((plane, ROWS, WIDTH), BF16))],
        [SMEM, SMEM, HBM, HBM, HBM, HBM],
        [
            pltpu.VMEM((half, WIDE), BF16),
            pltpu.VMEM((texts, WIDE), BF16),
            pltpu.VMEM((half, WIDE), BF16),
            pltpu.VMEM((half, texts), BF16),
            pltpu.VMEM((half, texts), BF16),
            pltpu.VMEM((half, WIDE), BF16),
            pltpu.VMEM((plane, ROWS, WIDTH), BF16),
            pltpu.SemaphoreType.DMA((4,)),
            pltpu.SemaphoreType.DMA((plane // far + 1,)),
        ],
        flops=8 * half * texts * WIDTH,
        bytes_accessed=6 * texts * WIDE,
    )(log_temp, bias, other, group_text, mine, in_hbm(coeffs))

    text_terms = lax.all_to_all(text_part, ("y_lo", "x"), 0, 0, tiled=True)
    got = swap_cores(give)
    blocks = lax.axis_size("z_hi")
    rows = blocks * ROWS
    split = WIDE // 2
    keep, left, right = call(
        fold,
        [(VMEM, shape((rows, WIDE), F32)), (VMEM, shape((rows, split), BF16)), (VMEM, shape((rows, WIDE - split), BF16))],
        [SMEM, VMEM, VMEM],
        bytes_accessed=16 * rows * WIDE,
    )(place_of("z_lo"), keep, got)
    left = lax.ppermute(left, COLUMN, [(i, i ^ 1) for i in range(column)])
    right = lax.ppermute(
        right, COLUMN, [(i, (i + (1 if i % 2 else -1)) % column) for i in range(column)]
    )
    (image_terms,) = call(
        last_fold,
        [(HBM, shape((blocks, ROWS, WIDE), BF16))],
        [VMEM, VMEM, VMEM],
        [pltpu.VMEM((blocks, ROWS, WIDE), BF16), pltpu.SemaphoreType.DMA((blocks,))],
        bytes_accessed=8 * rows * WIDE,
    )(keep, left, right)
    image_terms, text_terms = lax.optimization_barrier((image_terms, text_terms))
    text_terms = text_terms.reshape(near, far, ROWS, WIDTH)
    place = lax.axis_index("y_hi").astype(jnp.int32)
    text_keep, text_give = call(
        fold_text,
        [(VMEM, shape((far // 2, ROWS, WIDTH), F32)), (VMEM, shape((far // 2, ROWS, WIDTH), BF16))],
        [SMEM, VMEM],
        bytes_accessed=3 * texts * WIDTH,
    )((place % 2).reshape(1), text_terms)
    text_got = lax.ppermute(text_give, "y_hi", [(i, i ^ 1) for i in range(far)])
    text_keep, text_give = call(
        fold_text_again,
        [(VMEM, shape((ROWS, WIDTH), F32)), (VMEM, shape((ROWS, WIDTH), BF16))],
        [SMEM, VMEM, VMEM],
        bytes_accessed=10 * ROWS * WIDTH,
    )((place // 2).reshape(1), text_keep, text_got)
    text_got = lax.ppermute(text_give, "y_hi", [(i, i ^ 2) for i in range(far)])

    image_terms = lax.all_to_all(image_terms, "z_hi", 0, 0, tiled=True)

    (grad_text,) = call(
        finish_text,
        [(VMEM, shape((ROWS, WIDTH), F32))],
        [SMEM, VMEM, VMEM, VMEM],
        bytes_accessed=12 * ROWS * WIDTH,
    )(log_temp, text_embed, text_keep, text_got)
    grad_image, loss = call(
        functools.partial(finish_image, total),
        [(VMEM, shape((ROWS, WIDTH), F32)), (VMEM, shape((1, ROWS), F32))],
        [SMEM, VMEM, VMEM],
        bytes_accessed=2 * blocks * ROWS * WIDE,
    )(log_temp, image_embed, image_terms)
    return (grad_image, grad_text, loss.reshape(ROWS))


def solution(mesh):
    parts = Mesh(mesh.devices.reshape(4, 4, 2, 2, 8, 2), AXES)
    placed = (P(AXES, None), P(AXES, None), P(AXES), P(), P())
    return jax.shard_map(
        on_device,
        mesh=parts,
        in_specs=placed,
        out_specs=(P(AXES, None), P(AXES, None), P(AXES)),
        check_vma=False,
    )
```

```python
import functools

import jax
import jax.numpy as jnp
from jax import lax
from jax.experimental import pallas as pl
from jax.experimental.pallas import tpu as pltpu
from jax.sharding import Mesh, PartitionSpec as P

AXES = ("x", "y_hi", "core", "y_lo", "z_hi", "z_lo")
PLANE = ("x", "y_hi", "y_lo")
COLUMN = ("z_hi", "z_lo")
WIDTH = 1152
WIDE = WIDTH + 128
ROWS = 16
LABEL_BASE = 128
F32, BF16 = jnp.float32, jnp.bfloat16

VMEM = pl.BlockSpec(memory_space=pltpu.VMEM)
SMEM = pl.BlockSpec(memory_space=pltpu.SMEM)
HBM = pl.BlockSpec(memory_space=pltpu.HBM)


def call(kernel, outs, in_specs, scratch=(), flops=0, bytes_accessed=0, vmem=16):
    return pl.pallas_call(
        kernel,
        out_shape=[
            pltpu.HBM(shape.shape, shape.dtype) if spec is HBM else shape for spec, shape in outs
        ],
        in_specs=in_specs,
        out_specs=[spec for spec, _ in outs],
        scratch_shapes=list(scratch),
        compiler_params=pltpu.CompilerParams(vmem_limit_bytes=vmem * 1024 * 1024),
        cost_estimate=pl.CostEstimate(
            flops=flops, bytes_accessed=bytes_accessed, transcendentals=0
        ),
    )


def start(*copies):
    for copy in copies:
        copy.start()
    return copies


def wait(*copies):
    for copy in copies:
        copy.wait()


def unit_of(embed):
    values = embed.astype(F32)
    radius = jnp.sqrt(jnp.sum(values * values, axis=1, keepdims=True) + 1e-06)
    return values / radius, radius


def prepare(
    labels_ref, image_ref, text_ref, image_out, text_out, labels_now, image_now, text_now, text_wide, in_sem, out_sem
):
    labels_copy, image_copy, text_copy = start(
        pltpu.make_async_copy(labels_ref, labels_now, in_sem.at[0]),
        pltpu.make_async_copy(image_ref, image_now, in_sem.at[1]),
        pltpu.make_async_copy(text_ref, text_now, in_sem.at[2]),
    )
    wait(labels_copy)
    shape = (ROWS, 128)
    row = lax.broadcasted_iota(jnp.int32, shape, 0)
    lane = lax.broadcasted_iota(jnp.int32, shape, 1)
    label = jnp.zeros(shape, jnp.int32)
    for r in range(ROWS):
        label = jnp.where(row == r, labels_now[r], label)
    high, low = label >> 7, label & (LABEL_BASE - 1)
    norm = high * high + low * low
    norm_high, norm_low = norm >> 7, norm & (LABEL_BASE - 1)

    def features(values):
        out = jnp.zeros(shape, jnp.int32)
        for k, value in enumerate(values):
            out = jnp.where(lane == k, value, out)
        return out.astype(F32).astype(BF16)

    wait(text_copy)
    text_low = unit_of(text_now[...])[0].astype(BF16)
    marks = features((high, low, LABEL_BASE, 1, norm_high, norm_low))
    copies = text_wide.shape[0]
    for k in range(copies):
        text_wide[k, :, :WIDTH] = text_low
        text_wide[k, :, WIDTH:] = marks
    copies = start(
        *[
            pltpu.make_async_copy(text_wide, text_out.at[pl.ds(k * copies, copies)], out_sem.at[k])
            for k in range(text_out.shape[0] // copies)
        ]
    )
    wait(image_copy)
    image_out[:, :WIDTH] = unit_of(image_now[...])[0].astype(BF16)
    image_out[:, WIDTH:] = features((-2 * high, -2 * low, norm_high, norm_low, LABEL_BASE, 1))
    wait(*copies)


def dot(left, right, left_dim, right_dim):
    return lax.dot_general(
        left, right, (((left_dim,), (right_dim,)), ((), ())), preferred_element_type=F32
    )


def loss_pair(loss):
    lane = lax.broadcasted_iota(jnp.int32, (loss.shape[0], 128), 1)
    high = loss.astype(BF16).astype(F32)
    return jnp.where(lane == 0, high, jnp.where(lane == 1, loss - high, 0.0)).astype(BF16)


def half_tile(log_temp_ref, bias_ref, wide, text_wide):
    scale = jnp.exp(jnp.full((1, 1), log_temp_ref[0], F32))
    scores = scale * dot(wide[:, :WIDTH], text_wide[:, :WIDTH], 1, 1) + bias_ref[0]
    positive = dot(wide[:, WIDTH:], text_wide[:, WIDTH:], 1, 1) == 0.0
    small = jnp.exp(-jnp.abs(scores))
    losses = jnp.maximum(jnp.where(positive, -scores, scores), 0.0) + jnp.log(1.0 + small)
    sigmoid = jnp.where(scores >= 0.0, 1.0, small) / (1.0 + small)
    coeffs = (sigmoid - jnp.where(positive, 1.0, 0.0)).astype(BF16)
    return jnp.sum(losses, axis=1, keepdims=True), coeffs


def first_tile(
    log_temp_ref, bias_ref, mine, text, coeffs_out, keep_out, coeffs_now, keep_now, out_sem
):
    loss, coeffs = half_tile(log_temp_ref, bias_ref, mine, text)
    coeffs_now[...] = coeffs
    (coeffs_copy,) = start(pltpu.make_async_copy(coeffs_now, coeffs_out, out_sem.at[0]))
    keep_now[:, :WIDTH] = dot(coeffs, text[:, :WIDTH], 1, 0)
    keep_now[:, WIDTH:] = loss_lane(loss)
    (keep_copy,) = start(pltpu.make_async_copy(keep_now, keep_out, out_sem.at[1]))
    wait(coeffs_copy, keep_copy)


def second_tile(
    order, far, log_temp_ref, bias_ref, other, text_ref, mine_ref, coeffs_ref, give_out, text_out,
    text, mine, mine_coeffs, coeffs_now, give_now, text_now, in_sem, out_sem
):
    text_copy, mine_copy, coeffs_copy = start(
        pltpu.make_async_copy(text_ref, text, in_sem.at[0]),
        pltpu.make_async_copy(mine_ref, mine, in_sem.at[1]),
        pltpu.make_async_copy(coeffs_ref, mine_coeffs, in_sem.at[2]),
    )
    wait(text_copy)
    loss, coeffs = half_tile(log_temp_ref, bias_ref, other, text)
    coeffs_now[...] = coeffs
    give_now[:, :WIDTH] = dot(coeffs, text[:, :WIDTH], 1, 0).astype(BF16)
    give_now[:, WIDTH:] = loss_pair(loss)
    copies = list(start(pltpu.make_async_copy(give_now, give_out, out_sem.at[0])))
    wait(mine_copy, coeffs_copy)
    chunk = 8
    for first in range(0, len(order), chunk):
        columns = pl.ds(first * ROWS, chunk * ROWS)
        total = dot(mine_coeffs[:, columns], mine[:, :WIDTH], 0, 0)
        total += dot(coeffs_now[:, columns], other[:, :WIDTH], 0, 0)
        for k in range(chunk):
            text_now[order[first + k]] = total[k * ROWS : (k + 1) * ROWS].astype(BF16)
        places = sorted(order[first : first + chunk])
        for run in range(0, chunk, far):
            blocks = pl.ds(places[run], far)
            copies += start(
                pltpu.make_async_copy(text_now.at[blocks], text_out.at[blocks], out_sem.at[len(copies)])
            )
    wait(*copies)


def loss_lane(loss):
    lane = lax.broadcasted_iota(jnp.int32, (loss.shape[0], 128), 1)
    return jnp.where(lane == 0, loss, 0.0)


def fold(bit_ref, keep_ref, got_ref, keep_out, left_out, right_out):
    bit = bit_ref[0]
    split = left_out.shape[1]
    for pair in range(keep_out.shape[0] // ROWS):
        out = pl.ds(pair * ROWS, ROWS)
        for place in (bit, 1 - bit):
            rows = pl.ds((2 * pair + place) * ROWS, ROWS)
            terms = keep_ref[rows, :] + got_ref[rows, :].astype(F32)
            loss = jnp.sum(terms[:, WIDTH:], axis=1, keepdims=True)
            if place is bit:
                keep_out[out, :WIDTH] = terms[:, :WIDTH]
                keep_out[out, WIDTH:] = loss_lane(loss)
            else:
                left_out[out, :] = terms[:, :split].astype(BF16)
                right_out[out, : WIDTH - split] = terms[:, split:WIDTH].astype(BF16)
                right_out[out, WIDTH - split :] = loss_pair(loss)


def last_fold(keep_ref, left_ref, right_ref, part_out, out_ref, out_sem):
    copies = []
    split = left_ref.shape[1]
    for block in range(out_ref.shape[0]):
        rows = pl.ds(block * ROWS, ROWS)
        out_ref[block, :, :split] = (keep_ref[rows, :split] + left_ref[rows, :].astype(F32)).astype(BF16)
        terms = keep_ref[rows, split:] + right_ref[rows, :].astype(F32)
        out_ref[block, :, split:WIDTH] = terms[:, : WIDTH - split].astype(BF16)
        loss = jnp.sum(terms[:, WIDTH - split :], axis=1, keepdims=True)
        out_ref[block, :, WIDTH:] = loss_pair(loss)
        if block % 4 == 3:
            run = pl.ds(block - 3, 4)
            copies += start(
                pltpu.make_async_copy(out_ref.at[run], part_out.at[run], out_sem.at[block // 4])
            )
    wait(*copies)


def unproject(log_temp_ref, embed_ref, terms):
    scale = jnp.exp(jnp.full((1, 1), log_temp_ref[0], F32))
    unit, radius = unit_of(embed_ref[...])
    grad = scale * terms
    return (grad - unit * jnp.sum(unit * grad, axis=1, keepdims=True)) / radius


def fold_text(bit_ref, terms_ref, keep_out, give_out):
    bit = bit_ref[0]
    for pair in range(keep_out.shape[0]):
        for out_ref, place in ((keep_out, bit), (give_out, 1 - bit)):
            terms = terms_ref[0, 2 * pair + place].astype(F32)
            for k in range(1, terms_ref.shape[0]):
                terms += terms_ref[k, 2 * pair + place].astype(F32)
            out_ref[pair] = terms.astype(out_ref.dtype)


def fold_text_again(bit_ref, keep_ref, got_ref, keep_out, give_out):
    bit = bit_ref[0]
    keep_out[...] = keep_ref[bit] + got_ref[bit].astype(F32)
    give_out[...] = (keep_ref[1 - bit] + got_ref[1 - bit].astype(F32)).astype(BF16)


def finish_text(log_temp_ref, embed_ref, keep_ref, got_ref, grad_out):
    terms = keep_ref[...] + got_ref[...].astype(F32)
    grad_out[...] = unproject(log_temp_ref, embed_ref, terms)


def finish_image(total, log_temp_ref, embed_ref, terms_ref, grad_out, loss_out):
    terms = terms_ref[0].astype(F32)
    for k in range(1, terms_ref.shape[0]):
        terms += terms_ref[k].astype(F32)
    grad_out[...] = unproject(log_temp_ref, embed_ref, terms[:, :WIDTH])
    loss = jnp.sum(terms[:, WIDTH:], axis=1, keepdims=True) / total
    row = lax.broadcasted_iota(jnp.int32, (ROWS, 128), 0)
    lane = lax.broadcasted_iota(jnp.int32, (ROWS, 128), 1)
    loss_out[...] = jnp.sum(jnp.where(row == lane, loss, 0.0), axis=0, keepdims=True)[:, :ROWS]


def in_hbm(array):
    return pltpu.with_memory_space_constraint(array, pltpu.HBM)


def place_of(axis):
    return lax.axis_index(axis).astype(jnp.int32).reshape(1)


def swap_cores(part):
    return lax.ppermute(part, "core", [(0, 1), (1, 0)])


def on_device(image_embed, text_embed, labels, log_temp, bias):
    total = ROWS * lax.axis_size(AXES)
    plane, column = lax.axis_size(PLANE), lax.axis_size(COLUMN)
    shape = jax.ShapeDtypeStruct

    image_wide, text_wide = call(
        prepare,
        [(VMEM, shape((ROWS, WIDE), BF16)), (HBM, shape((plane, ROWS, WIDE), BF16))],
        [HBM, HBM, HBM],
        [
            pltpu.SMEM((ROWS,), jnp.int32),
            pltpu.VMEM((ROWS, WIDTH), BF16),
            pltpu.VMEM((ROWS, WIDTH), BF16),
            pltpu.VMEM((8, ROWS, WIDE), BF16),
            pltpu.SemaphoreType.DMA((3,)),
            pltpu.SemaphoreType.DMA((plane // 8,)),
        ],
        bytes_accessed=plane * ROWS * WIDE * 2,
    )(in_hbm(labels), in_hbm(image_embed), in_hbm(text_embed))

    group_text = lax.all_to_all(text_wide, PLANE, 0, 0, tiled=True).reshape(-1, WIDE)
    mine = lax.all_gather(image_wide, COLUMN, axis=0, tiled=True)
    other = swap_cores(mine)

    half, texts = column * ROWS, plane * ROWS

    coeffs, keep = call(
        first_tile,
        [(HBM, shape((half, texts), BF16)), (HBM, shape((half, WIDE), F32))],
        [SMEM, SMEM, VMEM, VMEM],
        [
            pltpu.VMEM((half, texts), BF16),
            pltpu.VMEM((half, WIDE), F32),
            pltpu.SemaphoreType.DMA((2,)),
        ],
        flops=4 * half * texts * WIDTH,
        bytes_accessed=4 * texts * WIDE,
    )(log_temp, bias, mine, group_text)

    far, low = lax.axis_size("y_hi"), lax.axis_size("y_lo")
    near = plane // far
    wide = plane // far // low
    order = [((b % low) * wide + b // low // far) * far + (b // low) % far for b in range(plane)]
    give, text_part = call(
        functools.partial(second_tile, order, far),
        [(HBM, shape((half, WIDE), BF16)), (HBM, shape((plane, ROWS, WIDTH), BF16))],
        [SMEM, SMEM, VMEM, HBM, HBM, HBM],
        [
            pltpu.VMEM((texts, WIDE), BF16),
            pltpu.VMEM((half, WIDE), BF16),
            pltpu.VMEM((half, texts), BF16),
            pltpu.VMEM((half, texts), BF16),
            pltpu.VMEM((half, WIDE), BF16),
            pltpu.VMEM((plane, ROWS, WIDTH), BF16),
            pltpu.SemaphoreType.DMA((3,)),
            pltpu.SemaphoreType.DMA((plane // far + 1,)),
        ],
        flops=8 * half * texts * WIDTH,
        bytes_accessed=6 * texts * WIDE,
    )(log_temp, bias, other, group_text, mine, in_hbm(coeffs))

    text_terms = lax.all_to_all(text_part, ("y_lo", "x"), 0, 0, tiled=True)
    got = swap_cores(give)
    blocks = lax.axis_size("z_hi")
    rows = blocks * ROWS
    split = WIDE // 2
    keep, left, right = call(
        fold,
        [(VMEM, shape((rows, WIDE), F32)), (VMEM, shape((rows, split), BF16)), (VMEM, shape((rows, WIDE - split), BF16))],
        [SMEM, VMEM, VMEM],
        bytes_accessed=16 * rows * WIDE,
    )(place_of("z_lo"), keep, got)
    left = lax.ppermute(left, COLUMN, [(i, i ^ 1) for i in range(column)])
    right = lax.ppermute(
        right, COLUMN, [(i, (i + (1 if i % 2 else -1)) % column) for i in range(column)]
    )
    (image_terms,) = call(
        last_fold,
        [(HBM, shape((blocks, ROWS, WIDE), BF16))],
        [VMEM, VMEM, VMEM],
        [pltpu.VMEM((blocks, ROWS, WIDE), BF16), pltpu.SemaphoreType.DMA((blocks // 4,))],
        bytes_accessed=8 * rows * WIDE,
    )(keep, left, right)
    image_terms, text_terms = lax.optimization_barrier((image_terms, text_terms))
    text_terms = text_terms.reshape(near, far, ROWS, WIDTH)
    place = lax.axis_index("y_hi").astype(jnp.int32)
    text_keep, text_give = call(
        fold_text,
        [(VMEM, shape((far // 2, ROWS, WIDTH), F32)), (VMEM, shape((far // 2, ROWS, WIDTH), BF16))],
        [SMEM, VMEM],
        bytes_accessed=3 * texts * WIDTH,
    )((place % 2).reshape(1), text_terms)
    text_got = lax.ppermute(text_give, "y_hi", [(i, i ^ 1) for i in range(far)])
    text_keep, text_give = call(
        fold_text_again,
        [(VMEM, shape((ROWS, WIDTH), F32)), (VMEM, shape((ROWS, WIDTH), BF16))],
        [SMEM, VMEM, VMEM],
        bytes_accessed=10 * ROWS * WIDTH,
    )((place // 2).reshape(1), text_keep, text_got)
    text_got = lax.ppermute(text_give, "y_hi", [(i, i ^ 2) for i in range(far)])

    image_terms = lax.all_to_all(image_terms, "z_hi", 0, 0, tiled=True)

    (grad_text,) = call(
        finish_text,
        [(VMEM, shape((ROWS, WIDTH), F32))],
        [SMEM, VMEM, VMEM, VMEM],
        bytes_accessed=12 * ROWS * WIDTH,
    )(log_temp, text_embed, text_keep, text_got)
    grad_image, loss = call(
        functools.partial(finish_image, total),
        [(VMEM, shape((ROWS, WIDTH), F32)), (VMEM, shape((1, ROWS), F32))],
        [SMEM, VMEM, VMEM],
        bytes_accessed=2 * blocks * ROWS * WIDE,
    )(log_temp, image_embed, image_terms)
    return (grad_image, grad_text, loss.reshape(ROWS))


def solution(mesh):
    parts = Mesh(mesh.devices.reshape(4, 4, 2, 2, 8, 2), AXES)
    placed = (P(AXES, None), P(AXES, None), P(AXES), P(), P())
    return jax.shard_map(
        on_device,
        mesh=parts,
        in_specs=placed,
        out_specs=(P(AXES, None), P(AXES, None), P(AXES)),
        check_vma=False,
    )
```

```python
import functools

import jax
import jax.numpy as jnp
from jax import lax
from jax.experimental import pallas as pl
from jax.experimental.pallas import tpu as pltpu
from jax.sharding import Mesh, PartitionSpec as P

AXES = ("x", "y_hi", "core", "y_lo", "z_hi", "z_lo")
PLANE = ("x", "y_lo", "y_hi")
COLUMN = ("z_hi", "z_lo")
WIDTH = 1152
WIDE = WIDTH + 128
ROWS = 16
LABEL_BASE = 128
F32, BF16 = jnp.float32, jnp.bfloat16

VMEM = pl.BlockSpec(memory_space=pltpu.VMEM)
SMEM = pl.BlockSpec(memory_space=pltpu.SMEM)
HBM = pl.BlockSpec(memory_space=pltpu.HBM)


def call(kernel, outs, in_specs, scratch=(), flops=0, bytes_accessed=0, vmem=16):
    return pl.pallas_call(
        kernel,
        out_shape=[
            pltpu.HBM(shape.shape, shape.dtype) if spec is HBM else shape for spec, shape in outs
        ],
        in_specs=in_specs,
        out_specs=[spec for spec, _ in outs],
        scratch_shapes=list(scratch),
        compiler_params=pltpu.CompilerParams(vmem_limit_bytes=vmem * 1024 * 1024),
        cost_estimate=pl.CostEstimate(
            flops=flops, bytes_accessed=bytes_accessed, transcendentals=0
        ),
    )


def start(*copies):
    for copy in copies:
        copy.start()
    return copies


def wait(*copies):
    for copy in copies:
        copy.wait()


def unit_of(embed):
    values = embed.astype(F32)
    radius = jnp.sqrt(jnp.sum(values * values, axis=1, keepdims=True) + 1e-06)
    return values / radius, radius


def prepare(
    labels_ref, image_ref, text_ref, image_out, text_out, labels_now, image_now, text_now, text_wide, in_sem, out_sem
):
    labels_copy, image_copy, text_copy = start(
        pltpu.make_async_copy(labels_ref, labels_now, in_sem.at[0]),
        pltpu.make_async_copy(image_ref, image_now, in_sem.at[1]),
        pltpu.make_async_copy(text_ref, text_now, in_sem.at[2]),
    )
    wait(labels_copy)
    shape = (ROWS, 128)
    row = lax.broadcasted_iota(jnp.int32, shape, 0)
    lane = lax.broadcasted_iota(jnp.int32, shape, 1)
    label = jnp.zeros(shape, jnp.int32)
    for r in range(ROWS):
        label = jnp.where(row == r, labels_now[r], label)
    high, low = label >> 7, label & (LABEL_BASE - 1)
    norm = high * high + low * low
    norm_high, norm_low = norm >> 7, norm & (LABEL_BASE - 1)

    def features(values):
        out = jnp.zeros(shape, jnp.int32)
        for k, value in enumerate(values):
            out = jnp.where(lane == k, value, out)
        return out.astype(F32).astype(BF16)

    wait(text_copy)
    text_low = unit_of(text_now[...])[0].astype(BF16)
    marks = features((high, low, LABEL_BASE, 1, norm_high, norm_low))
    copies = text_wide.shape[0]
    for k in range(copies):
        text_wide[k, :, :WIDTH] = text_low
        text_wide[k, :, WIDTH:] = marks
    copies = start(
        *[
            pltpu.make_async_copy(text_wide, text_out.at[pl.ds(k * copies, copies)], out_sem.at[k])
            for k in range(text_out.shape[0] // copies)
        ]
    )
    wait(image_copy)
    image_out[:, :WIDTH] = unit_of(image_now[...])[0].astype(BF16)
    image_out[:, WIDTH:] = features((-2 * high, -2 * low, norm_high, norm_low, LABEL_BASE, 1))
    wait(*copies)


def dot(left, right, left_dim, right_dim):
    return lax.dot_general(
        left, right, (((left_dim,), (right_dim,)), ((), ())), preferred_element_type=F32
    )


def loss_pair(loss):
    lane = lax.broadcasted_iota(jnp.int32, (loss.shape[0], 128), 1)
    high = loss.astype(BF16).astype(F32)
    return jnp.where(lane == 0, high, jnp.where(lane == 1, loss - high, 0.0)).astype(BF16)


def half_tile(log_temp_ref, bias_ref, wide, text_wide):
    scale = jnp.exp(jnp.full((1, 1), log_temp_ref[0], F32))
    scores = scale * dot(wide[:, :WIDTH], text_wide[:, :WIDTH], 1, 1) + bias_ref[0]
    positive = dot(wide[:, WIDTH:], text_wide[:, WIDTH:], 1, 1) == 0.0
    small = jnp.exp(-jnp.abs(scores))
    losses = jnp.maximum(jnp.where(positive, -scores, scores), 0.0) + jnp.log(1.0 + small)
    sigmoid = jnp.where(scores >= 0.0, 1.0, small) / (1.0 + small)
    coeffs = (sigmoid - jnp.where(positive, 1.0, 0.0)).astype(BF16)
    return jnp.sum(losses, axis=1, keepdims=True), coeffs


def first_tile(
    log_temp_ref, bias_ref, mine, text, coeffs_out, keep_out, coeffs_now, keep_now, out_sem
):
    loss, coeffs = half_tile(log_temp_ref, bias_ref, mine, text)
    coeffs_now[...] = coeffs
    (coeffs_copy,) = start(pltpu.make_async_copy(coeffs_now, coeffs_out, out_sem.at[0]))
    keep_now[:, :WIDTH] = dot(coeffs, text[:, :WIDTH], 1, 0)
    keep_now[:, WIDTH:] = loss_lane(loss)
    (keep_copy,) = start(pltpu.make_async_copy(keep_now, keep_out, out_sem.at[1]))
    wait(coeffs_copy, keep_copy)


def second_tile(
    order, far, log_temp_ref, bias_ref, other_ref, text_ref, mine_ref, coeffs_ref, give_out, text_out,
    other, text, mine, mine_coeffs, coeffs_now, give_now, text_now, in_sem, out_sem
):
    other_copy, text_copy, mine_copy, coeffs_copy = start(
        pltpu.make_async_copy(other_ref, other, in_sem.at[0]),
        pltpu.make_async_copy(text_ref, text, in_sem.at[1]),
        pltpu.make_async_copy(mine_ref, mine, in_sem.at[2]),
        pltpu.make_async_copy(coeffs_ref, mine_coeffs, in_sem.at[3]),
    )
    wait(other_copy, text_copy)
    loss, coeffs = half_tile(log_temp_ref, bias_ref, other, text)
    coeffs_now[...] = coeffs
    give_now[:, :WIDTH] = dot(coeffs, text[:, :WIDTH], 1, 0).astype(BF16)
    give_now[:, WIDTH:] = loss_pair(loss)
    copies = list(start(pltpu.make_async_copy(give_now, give_out, out_sem.at[0])))
    wait(mine_copy, coeffs_copy)
    chunk = 8
    for first in range(0, len(order), chunk):
        columns = pl.ds(first * ROWS, chunk * ROWS)
        total = dot(mine_coeffs[:, columns], mine[:, :WIDTH], 0, 0)
        total += dot(coeffs_now[:, columns], other[:, :WIDTH], 0, 0)
        for k in range(chunk):
            text_now[order[first + k]] = total[k * ROWS : (k + 1) * ROWS].astype(BF16)
        places = sorted(order[first : first + chunk])
        for run in range(0, chunk, far):
            blocks = pl.ds(places[run], far)
            copies += start(
                pltpu.make_async_copy(text_now.at[blocks], text_out.at[blocks], out_sem.at[len(copies)])
            )
    wait(*copies)


def loss_lane(loss):
    lane = lax.broadcasted_iota(jnp.int32, (loss.shape[0], 128), 1)
    return jnp.where(lane == 0, loss, 0.0)


def fold(bit_ref, keep_ref, got_ref, keep_out, left_out, right_out):
    bit = bit_ref[0]
    split = left_out.shape[1]
    for pair in range(keep_out.shape[0] // ROWS):
        out = pl.ds(pair * ROWS, ROWS)
        for place in (bit, 1 - bit):
            rows = pl.ds((2 * pair + place) * ROWS, ROWS)
            terms = keep_ref[rows, :] + got_ref[rows, :].astype(F32)
            loss = jnp.sum(terms[:, WIDTH:], axis=1, keepdims=True)
            if place is bit:
                keep_out[out, :WIDTH] = terms[:, :WIDTH]
                keep_out[out, WIDTH:] = loss_lane(loss)
            else:
                left_out[out, :] = terms[:, :split].astype(BF16)
                right_out[out, : WIDTH - split] = terms[:, split:WIDTH].astype(BF16)
                right_out[out, WIDTH - split :] = loss_pair(loss)


def last_fold(keep_ref, left_ref, right_ref, part_out, out_ref, out_sem):
    copies = []
    split = left_ref.shape[1]
    for block in range(out_ref.shape[0]):
        rows = pl.ds(block * ROWS, ROWS)
        out_ref[block, :, :split] = (keep_ref[rows, :split] + left_ref[rows, :].astype(F32)).astype(BF16)
        terms = keep_ref[rows, split:] + right_ref[rows, :].astype(F32)
        out_ref[block, :, split:WIDTH] = terms[:, : WIDTH - split].astype(BF16)
        loss = jnp.sum(terms[:, WIDTH - split :], axis=1, keepdims=True)
        out_ref[block, :, WIDTH:] = loss_pair(loss)
        copies += start(
            pltpu.make_async_copy(out_ref.at[block], part_out.at[block], out_sem.at[block])
        )
    wait(*copies)


def unproject(log_temp_ref, embed_ref, terms):
    scale = jnp.exp(jnp.full((1, 1), log_temp_ref[0], F32))
    unit, radius = unit_of(embed_ref[...])
    grad = scale * terms
    return (grad - unit * jnp.sum(unit * grad, axis=1, keepdims=True)) / radius


def fold_text(bit_ref, terms_ref, keep_out, give_out):
    bit = bit_ref[0]
    for pair in range(keep_out.shape[0]):
        for out_ref, place in ((keep_out, bit), (give_out, 1 - bit)):
            terms = terms_ref[0, 2 * pair + place].astype(F32)
            for k in range(1, terms_ref.shape[0]):
                terms += terms_ref[k, 2 * pair + place].astype(F32)
            out_ref[pair] = terms.astype(out_ref.dtype)


def fold_text_again(bit_ref, keep_ref, got_ref, keep_out, give_out):
    bit = bit_ref[0]
    keep_out[...] = keep_ref[bit] + got_ref[bit].astype(F32)
    give_out[...] = (keep_ref[1 - bit] + got_ref[1 - bit].astype(F32)).astype(BF16)


def finish_text(log_temp_ref, embed_ref, keep_ref, got_ref, grad_out):
    terms = keep_ref[...] + got_ref[...].astype(F32)
    grad_out[...] = unproject(log_temp_ref, embed_ref, terms)


def finish_image(total, log_temp_ref, embed_ref, terms_ref, grad_out, loss_out):
    terms = terms_ref[0].astype(F32)
    for k in range(1, terms_ref.shape[0]):
        terms += terms_ref[k].astype(F32)
    grad_out[...] = unproject(log_temp_ref, embed_ref, terms[:, :WIDTH])
    loss = jnp.sum(terms[:, WIDTH:], axis=1, keepdims=True) / total
    row = lax.broadcasted_iota(jnp.int32, (ROWS, 128), 0)
    lane = lax.broadcasted_iota(jnp.int32, (ROWS, 128), 1)
    loss_out[...] = jnp.sum(jnp.where(row == lane, loss, 0.0), axis=0, keepdims=True)[:, :ROWS]


def in_hbm(array):
    return pltpu.with_memory_space_constraint(array, pltpu.HBM)


def place_of(axis):
    return lax.axis_index(axis).astype(jnp.int32).reshape(1)


def swap_cores(part):
    return lax.ppermute(part, "core", [(0, 1), (1, 0)])


def on_device(image_embed, text_embed, labels, log_temp, bias):
    total = ROWS * lax.axis_size(AXES)
    plane, column = lax.axis_size(PLANE), lax.axis_size(COLUMN)
    shape = jax.ShapeDtypeStruct

    image_wide, text_wide = call(
        prepare,
        [(VMEM, shape((ROWS, WIDE), BF16)), (HBM, shape((plane, ROWS, WIDE), BF16))],
        [HBM, HBM, HBM],
        [
            pltpu.SMEM((ROWS,), jnp.int32),
            pltpu.VMEM((ROWS, WIDTH), BF16),
            pltpu.VMEM((ROWS, WIDTH), BF16),
            pltpu.VMEM((8, ROWS, WIDE), BF16),
            pltpu.SemaphoreType.DMA((3,)),
            pltpu.SemaphoreType.DMA((plane // 8,)),
        ],
        bytes_accessed=plane * ROWS * WIDE * 2,
    )(in_hbm(labels), in_hbm(image_embed), in_hbm(text_embed))

    group_text = lax.all_to_all(text_wide, PLANE, 0, 0, tiled=True).reshape(-1, WIDE)
    mine = lax.all_gather(image_wide, COLUMN, axis=0, tiled=True)
    other = swap_cores(mine)

    half, texts = column * ROWS, plane * ROWS

    coeffs, keep = call(
        first_tile,
        [(HBM, shape((half, texts), BF16)), (HBM, shape((half, WIDE), F32))],
        [SMEM, SMEM, VMEM, VMEM],
        [
            pltpu.VMEM((half, texts), BF16),
            pltpu.VMEM((half, WIDE), F32),
            pltpu.SemaphoreType.DMA((2,)),
        ],
        flops=4 * half * texts * WIDTH,
        bytes_accessed=4 * texts * WIDE,
    )(log_temp, bias, mine, group_text)

    far, low = lax.axis_size("y_hi"), lax.axis_size("y_lo")
    near = plane // far
    wide = plane // far // low
    order = [(b // far % low * wide + b // far // low) * far + b % far for b in range(plane)]
    give, text_part = call(
        functools.partial(second_tile, order, far),
        [(HBM, shape((half, WIDE), BF16)), (HBM, shape((plane, ROWS, WIDTH), BF16))],
        [SMEM, SMEM, HBM, HBM, HBM, HBM],
        [
            pltpu.VMEM((half, WIDE), BF16),
            pltpu.VMEM((texts, WIDE), BF16),
            pltpu.VMEM((half, WIDE), BF16),
            pltpu.VMEM((half, texts), BF16),
            pltpu.VMEM((half, texts), BF16),
            pltpu.VMEM((half, WIDE), BF16),
            pltpu.VMEM((plane, ROWS, WIDTH), BF16),
            pltpu.SemaphoreType.DMA((4,)),
            pltpu.SemaphoreType.DMA((plane // far + 1,)),
        ],
        flops=8 * half * texts * WIDTH,
        bytes_accessed=6 * texts * WIDE,
    )(log_temp, bias, other, group_text, mine, in_hbm(coeffs))

    text_terms = lax.all_to_all(text_part, ("y_lo", "x"), 0, 0, tiled=True)
    got = swap_cores(give)
    blocks = lax.axis_size("z_hi")
    rows = blocks * ROWS
    split = WIDE // 2
    keep, left, right = call(
        fold,
        [(VMEM, shape((rows, WIDE), F32)), (VMEM, shape((rows, split), BF16)), (VMEM, shape((rows, WIDE - split), BF16))],
        [SMEM, VMEM, VMEM],
        bytes_accessed=16 * rows * WIDE,
    )(place_of("z_lo"), keep, got)
    left = lax.ppermute(left, COLUMN, [(i, i ^ 1) for i in range(column)])
    right = lax.ppermute(
        right, COLUMN, [(i, (i + (1 if i % 2 else -1)) % column) for i in range(column)]
    )
    (image_terms,) = call(
        last_fold,
        [(HBM, shape((blocks, ROWS, WIDE), BF16))],
        [VMEM, VMEM, VMEM],
        [pltpu.VMEM((blocks, ROWS, WIDE), BF16), pltpu.SemaphoreType.DMA((blocks,))],
        bytes_accessed=8 * rows * WIDE,
    )(keep, left, right)
    image_terms, text_terms = lax.optimization_barrier((image_terms, text_terms))
    text_terms = text_terms.reshape(near, far, ROWS, WIDTH)
    place = lax.axis_index("y_hi").astype(jnp.int32)
    text_keep, text_give = call(
        fold_text,
        [(VMEM, shape((far // 2, ROWS, WIDTH), F32)), (VMEM, shape((far // 2, ROWS, WIDTH), BF16))],
        [SMEM, VMEM],
        bytes_accessed=3 * texts * WIDTH,
    )((place % 2).reshape(1), text_terms)
    text_got = lax.ppermute(text_give, "y_hi", [(i, i ^ 1) for i in range(far)])
    text_keep, text_give = call(
        fold_text_again,
        [(VMEM, shape((ROWS, WIDTH), F32)), (VMEM, shape((ROWS, WIDTH), BF16))],
        [SMEM, VMEM, VMEM],
        bytes_accessed=10 * ROWS * WIDTH,
    )((place // 2).reshape(1), text_keep, text_got)
    text_got = lax.ppermute(text_give, "y_hi", [(i, i ^ 2) for i in range(far)])

    image_terms = lax.all_to_all(image_terms, "z_hi", 0, 0, tiled=True)

    (grad_text,) = call(
        finish_text,
        [(VMEM, shape((ROWS, WIDTH), F32))],
        [SMEM, VMEM, VMEM, VMEM],
        bytes_accessed=12 * ROWS * WIDTH,
    )(log_temp, text_embed, text_keep, text_got)
    grad_image, loss = call(
        functools.partial(finish_image, total),
        [(VMEM, shape((ROWS, WIDTH), F32)), (VMEM, shape((1, ROWS), F32))],
        [SMEM, VMEM, VMEM],
        bytes_accessed=2 * blocks * ROWS * WIDE,
    )(log_temp, image_embed, image_terms)
    return (grad_image, grad_text, loss.reshape(ROWS))


def solution(mesh):
    parts = Mesh(mesh.devices.reshape(4, 4, 2, 2, 8, 2), AXES)
    placed = (P(AXES, None), P(AXES, None), P(AXES), P(), P())
    return jax.shard_map(
        on_device,
        mesh=parts,
        in_specs=placed,
        out_specs=(P(AXES, None), P(AXES, None), P(AXES)),
        check_vma=False,
    )
```
